32 devices in a mesh: bulk: 4 (over y, core), col: 8 (over z, x).
Axes of the slice: x: 2, y: 2, z: 4, core: 2. Of those that a mesh axis runs over, the one named last changes fastest.
Arguments:
- parent_front: float32 [16384, 16384], P('bulk', 'col'), may hold values from -4 to 4
- child_blocks: bfloat16 [4096, 128, 128], P(('bulk', 'col')), may hold values from -4 to 4
- child_owner: int32 [4096, 1], P(('bulk', 'col')), may hold values from 0 to 31; in each aligned block of 128 rows (0 to 127, 128 to 255, ...) at most 8 rows name the same one
- child_slot: int32 [4096], P(('bulk', 'col')), may hold values from 0 to 511
- pivot_inverse: float32 [512, 512], replicated, may hold values from -0.25 to 0.25
Outputs:
- factored_front: float32 [16384, 16384], P('bulk', 'col')
The draws below stay inside these ranges and needn't reach their ends.
Inputs may be any that keep to these rules, and one draw needn't show every extreme that they name: `child_owner`: of the 128 child blocks of one device, at most 8 name the same owner; in every draw some device sends exactly 8 to some owner.
All inputs are finite; a program needn't handle non-finite values.
Results may differ from the reference program's by a relative error of at most 0.0003.
Values may be sent and summed in bfloat16 or wider, within the bound.
No kernel may reach another device: no remote copies, remote signals or barrier semaphores. Data moves between devices by JAX's collectives and lax.ppermute only.
A program may use at most 192 MiB of HBM per device.

```python
import math
import jax
import jax.numpy as jnp
import numpy as np
from jax import lax

F = 16384
PW = 512
BS = 128
NB_DEV = 128
CAP = 8
CHILDREN = 4096
RB_DEV = 32
CB_DEV = 16
LOCAL_BLOCKS = 512
N_COL = 8
DEVICES = 32


def plant(entries, stream_key, low, high):
    longest = entries.shape.index(max(entries.shape))
    spots = []
    for shift in (0, 1):
        where = [jax.random.randint(jax.random.fold_in(stream_key, axis), (), 0, length) for axis, length in enumerate(entries.shape)]
        where[longest] = (where[longest] + shift) % entries.shape[longest]
        spots.append(tuple(where))
    return entries.at[spots[0]].set(low).at[spots[1]].set(high)


def block_scale(own_key, shape, split, smallest, largest):
    def one(axis_at, parts):
        draws = jax.random.uniform(jax.random.fold_in(jax.random.fold_in(own_key, 6), axis_at), (parts,), jnp.float32, smallest / len(split), largest / len(split))
        return jnp.repeat(jnp.exp(draws), shape[axis_at] // parts).reshape((-1,) + (1,) * (len(shape) - axis_at - 1))

    factor_of = one(*split[0])
    for cut in split[1:]:
        factor_of = factor_of * one(*cut)
    return factor_of


def shared_out(rng, own, number, rows, count, top, limit, skew):
    sequence = jax.random.permutation(rng, count)
    crowded, usual = load_shares(count, rows * top, limit, skew, True), load_shares(count, rows * top, limit, skew, False)
    places = jnp.arange(count)

    def named(sizes, rotation):
        used = int((sizes > 0).sum())
        fixed = max(1, used // 4)
        shifted = fixed + (places - fixed + rotation * (used - fixed)) % max(1, count - fixed)
        return jnp.zeros((count,), jnp.int32).at[sequence[jnp.where(places < fixed, places, shifted)]].set(jnp.asarray(sizes, jnp.int32))

    sizes = jnp.where(number % 4 == 0, named(crowded, number // 4), named(usual, number - number // 4 - 1))
    mixed = jax.random.permutation(jax.random.fold_in(own, 3), count)
    donor, receiver = mixed[0:count // 2 * 2:2], mixed[1:count // 2 * 2:2]
    slack = jnp.minimum(sizes[donor] - 1, limit - sizes[receiver]) // 2
    slack = jnp.where((donor == sequence[0]) | (receiver == sequence[0]) | (sizes[receiver] == 0), 0, jnp.maximum(slack, 0))
    shifted = jax.random.randint(jax.random.fold_in(own, 4), (count // 2,), 0, 1 << 20) % (slack + 1)
    sizes = sizes.at[donor].add(-shifted).at[receiver].add(shifted)
    labels = jnp.searchsorted(jnp.cumsum(sizes), jnp.arange(rows * top), side="right").astype(jnp.int32)
    listing = labels.reshape(top, rows).T
    listing = listing[jax.random.permutation(jax.random.fold_in(own, 1), rows)]
    rotation = jax.random.randint(jax.random.fold_in(own, 2), (rows, 1), 0, top)
    return jnp.take_along_axis(listing, (jnp.arange(top)[None, :] + rotation) % top, axis=1)


def load_shares(count, total, bound, lean, full):
    loads = [(1 << 20) // math.isqrt(standing ** lean) + 1 for standing in range(1, count + 1)]
    largest = bound if full else min(bound, max(-(-total // count), total * loads[0] // sum(loads)))
    least = 1 if total - largest >= count - 1 else 0
    counts, rest = [largest] + [least] * (count - 1), total - largest - least * (count - 1)
    while rest > 0:
        movable = [i for i in range(1, count) if counts[i] < largest] or [i for i in range(1, count) if counts[i] < bound]
        whole, budget = sum([loads[i] for i in movable]), rest
        for i in movable:
            extra = min(bound - counts[i], max(1, budget * loads[i] // whole), rest)
            counts[i] = counts[i] + extra
            rest = rest - extra
    return np.array(counts)


def bell_draw(own_key, shape, width, bound, cuts=(), held_as=jnp.bfloat16):
    result = width * jax.random.normal(own_key, shape, jnp.float32)
    if cuts:
        result = result * block_scale(own_key, shape, cuts, -0.22, 0.18)
    return jnp.clip(result, -bound, bound).astype(held_as)


def setup_inputs(seed: int = 0) -> dict:
    streams_of = jax.random.split(jax.random.key(seed), 6)
    parent_front = bell_draw(streams_of[0], (F, F), 0.3, 4.0, ((0, 4), (1, 8)), jnp.float32)
    child_blocks = bell_draw(streams_of[1], (CHILDREN, BS, BS), 0.3, 4.0, ((0, 32),))
    child_owner_keys = jax.random.split(jax.random.fold_in(streams_of[2], 1), CHILDREN // NB_DEV)
    child_owner_turns = jax.random.permutation(jax.random.fold_in(streams_of[2], 3), CHILDREN // NB_DEV)
    child_owner = jax.vmap(lambda own, number: shared_out(jax.random.fold_in(streams_of[2], 2), own, number, NB_DEV, DEVICES, 1, CAP, 2))(child_owner_keys, child_owner_turns).reshape((CHILDREN, 1))
    child_slot = plant(jax.random.randint(streams_of[3], (CHILDREN,), 0, LOCAL_BLOCKS), jax.random.fold_in(streams_of[3], 1), 0, LOCAL_BLOCKS - 1).astype(jnp.int32)
    pivot_inverse = bell_draw(streams_of[4], (PW, PW), PW ** -0.5, 0.25, (), jnp.float32)
    return dict(parent_front=parent_front, child_blocks=child_blocks, child_owner=child_owner, child_slot=child_slot, pivot_inverse=pivot_inverse)


def reference(parent_front, child_blocks, child_owner, child_slot, pivot_inverse):
    block_count = F // BS
    owner_index = child_owner[:, 0].astype(jnp.int32)
    block_row = (owner_index // N_COL) * RB_DEV + child_slot // CB_DEV
    block_column = (owner_index % N_COL) * CB_DEV + child_slot % CB_DEV
    tiles = parent_front.reshape(block_count, BS, block_count, BS).transpose(0, 2, 1, 3)
    tiles = tiles.at[block_row, block_column].add(child_blocks.astype(jnp.float32))
    extended = tiles.transpose(0, 2, 1, 3).reshape(F, F)
    highest = lax.Precision.HIGHEST
    lower = jnp.dot(extended[PW:, :PW], pivot_inverse, precision=highest)
    schur = extended[PW:, PW:] - jnp.dot(lower, extended[:PW, PW:], precision=highest)
    bottom = jnp.concatenate([lower, schur], axis=1)
    return jnp.concatenate([extended[:PW], bottom], axis=0)
```

```python
import functools

import jax
import jax.numpy as jnp
from jax import lax
from jax.experimental import pallas as pl
from jax.experimental.pallas import tpu as pltpu
from jax.sharding import PartitionSpec as P

PW = 512
TILE = 128
META = 16
CODE_TOP = 32600.0
VMEM_LIMIT = 56 * 1024 * 1024

F32 = jnp.float32
BF16 = jnp.bfloat16
I32 = jnp.int32


def compiler_params(semantics=None):
    return pltpu.CompilerParams(dimension_semantics=semantics, vmem_limit_bytes=VMEM_LIMIT)


def pack_kernel(devices, capacity, owner_ref, slot_ref, child_ref, out_ref, filled, slots, meta, sem, meta_sem):
    child_count = owner_ref.shape[0]

    def clear(d, _):
        filled[d] = 0
        return 0

    lax.fori_loop(0, devices, clear, 0)

    def clear_slot(i, _):
        slots[i] = -1
        return 0

    lax.fori_loop(0, devices * capacity, clear_slot, 0)

    def place(i, _):
        d = owner_ref[i]
        k = filled[d]
        filled[d] = k + 1
        slots[d * capacity + k] = slot_ref[i]
        pltpu.make_async_copy(
            child_ref.at[i], out_ref.at[d, pl.ds(pl.multiple_of(k * TILE, TILE), TILE)], sem
        ).start()
        return 0

    lax.fori_loop(0, child_count, place, 0)
    lane = lax.broadcasted_iota(I32, (META, TILE), 1)
    row = lax.broadcasted_iota(I32, (META, TILE), 0)

    def write_meta(d, _):
        value = jnp.full((META, TILE), -1, I32)
        for k in range(capacity):
            value = jnp.where(lane == k, slots[d * capacity + k], value)
        coded = jnp.where(row == 0, value >> 4, value & 15)
        meta[d] = coded.astype(F32).astype(BF16)
        return 0

    lax.fori_loop(0, devices, write_meta, 0)
    copy = pltpu.make_async_copy(meta, out_ref.at[:, pl.ds(capacity * TILE, META)], meta_sem)
    copy.start()
    pltpu.make_async_copy(child_ref, child_ref, sem).wait()
    copy.wait()


def pack(owner, slot, child, devices, capacity):
    rows = capacity * TILE + META
    return pl.pallas_call(
        functools.partial(pack_kernel, devices, capacity),
        out_shape=jax.ShapeDtypeStruct((devices, rows, TILE), BF16),
        in_specs=[
            pl.BlockSpec(memory_space=pltpu.SMEM),
            pl.BlockSpec(memory_space=pltpu.SMEM),
            pl.BlockSpec(memory_space=pl.ANY),
        ],
        out_specs=pl.BlockSpec(memory_space=pl.ANY),
        scratch_shapes=[
            pltpu.SMEM((devices,), I32),
            pltpu.SMEM((devices * capacity,), I32),
            pltpu.VMEM((devices, META, TILE), BF16),
            pltpu.SemaphoreType.DMA,
            pltpu.SemaphoreType.DMA,
        ],
        compiler_params=compiler_params(),
        name="pack_children",
    )(owner, slot, child)


def read_slots(arrived, capacity):
    coded = arrived[:, capacity * TILE : capacity * TILE + 2, :capacity].astype(I32)
    return (coded[:, 0] * 16 + coded[:, 1]).reshape(-1)


def build_lists(key_ref, head, following, width):
    def clear(i, _):
        head[i] = -1
        return 0

    lax.fori_loop(0, head.shape[0], clear, 0)

    def add(i, _):
        key = key_ref[i]

        @pl.when(key >= 0)
        def _():
            strip = key // width
            following[i] = head[strip]
            head[strip] = i

        return 0

    lax.fori_loop(0, key_ref.shape[0], add, 0)


def add_strip(key_ref, arrived_ref, out, head, following, strip, width, capacity, row):
    def body(i):
        column = pl.multiple_of((key_ref[i] % width) * TILE, TILE)
        start = pl.multiple_of((i % capacity) * TILE, TILE)
        block = arrived_ref[i // capacity, pl.ds(start, TILE), :]
        spot = (pl.ds(row, TILE), pl.ds(column, TILE))
        out[spot] = out[spot] + block.astype(F32)
        return following[i]

    lax.while_loop(lambda i: i >= 0, body, head[strip])


def extend_kernel(width, capacity, key_ref, base_ref, arrived_ref, out_ref, head, following):
    step = pl.program_id(0)

    @pl.when(step == 0)
    def _():
        build_lists(key_ref, head, following, width)

    out_ref[...] = base_ref[...]
    strips = base_ref.shape[0] // TILE
    for s in range(strips):
        add_strip(
            key_ref, arrived_ref, out_ref, head, following, step * strips + s, width, capacity, s * TILE
        )


def extend(base, arrived, key, width, capacity, rows, columns, alias=False):
    return pl.pallas_call(
        functools.partial(extend_kernel, width, capacity),
        out_shape=jax.ShapeDtypeStruct((rows, columns), F32),
        grid_spec=pltpu.PrefetchScalarGridSpec(
            num_scalar_prefetch=1,
            grid=(rows // TILE,),
            in_specs=[
                pl.BlockSpec((TILE, columns), lambda i, k: (i, 0)),
                pl.BlockSpec(memory_space=pltpu.VMEM),
            ],
            out_specs=pl.BlockSpec((TILE, columns), lambda i, k: (i, 0)),
            scratch_shapes=[
                pltpu.SMEM((rows // TILE,), I32),
                pltpu.SMEM((key.shape[0],), I32),
            ],
        ),
        input_output_aliases={1: 0} if alias else {},
        compiler_params=compiler_params(("arbitrary",)),
        name="extend_add",
    )(key, base, arrived)


def code_rows(values):
    top = jnp.maximum(jnp.max(jnp.abs(values), axis=1, keepdims=True), 1e-30)
    exponent = jnp.ceil(jnp.log2(top) * 64.0)
    code = jnp.round(values * (CODE_TOP * jnp.exp2(exponent * (-1.0 / 64.0))))
    return code.astype(I32), exponent


def diagonal(n):
    return lax.broadcasted_iota(I32, (n, n), 0) == lax.broadcasted_iota(I32, (n, n), 1)


def panel_kernel(width, capacity, key_ref, base_ref, arrived_ref, out_ref, work, head, following):
    step = pl.program_id(0)

    @pl.when(step == 0)
    def _():
        build_lists(key_ref, head, following, width)

    work[...] = base_ref[...]
    rows = base_ref.shape[0]
    strips = rows // TILE
    eye = diagonal(TILE)
    out_ref[0, pl.ds(rows, META), :] = jnp.zeros((META, out_ref.shape[2]), jnp.int16)
    for s in range(strips):
        add_strip(
            key_ref, arrived_ref, work, head, following, step * strips + s, width, capacity, s * TILE
        )
        code, exponent = code_rows(work[pl.ds(s * TILE, TILE), :])
        out_ref[0, pl.ds(s * TILE, TILE), :] = code.astype(jnp.int16)
        line = jnp.sum(jnp.where(eye, exponent, 0.0), axis=0, keepdims=True)
        out_ref[0, pl.ds(rows, META), pl.ds(s * TILE, TILE)] = (
            jnp.broadcast_to(line, (META, TILE)).astype(I32).astype(jnp.int16)
        )


def code_panel(base, arrived, key, capacity, slices):
    rows = base.shape[0] // slices
    width = PW // TILE
    return pl.pallas_call(
        functools.partial(panel_kernel, width, capacity),
        out_shape=jax.ShapeDtypeStruct((slices, rows + META, PW), jnp.int16),
        grid_spec=pltpu.PrefetchScalarGridSpec(
            num_scalar_prefetch=1,
            grid=(slices,),
            in_specs=[
                pl.BlockSpec((rows, PW), lambda i, k: (i, 0)),
                pl.BlockSpec(memory_space=pltpu.VMEM),
            ],
            out_specs=pl.BlockSpec((1, rows + META, PW), lambda i, k: (i, 0, 0)),
            scratch_shapes=[
                pltpu.VMEM((rows, PW), F32),
                pltpu.SMEM((base.shape[0] // TILE,), I32),
                pltpu.SMEM((key.shape[0],), I32),
            ],
        ),
        compiler_params=compiler_params(("arbitrary",)),
        name="code_panel",
    )(key, base, arrived)


def right_kernel(flag_ref, pivot_ref, upper_ref, high_ref, low_ref):
    step = pl.program_id(0)
    columns = upper_ref.shape[1]
    row = lax.broadcasted_iota(I32, (PW, columns), 0)
    column = lax.broadcasted_iota(I32, (PW, columns), 1) + step * columns
    in_panel = jnp.logical_and(column < PW, flag_ref[1] == 0)
    upper = jnp.where(in_panel, jnp.where(row == column, -1.0, 0.0), upper_ref[...])
    right = jnp.dot(pivot_ref[...], upper, precision=lax.Precision.HIGHEST, preferred_element_type=F32)
    high = right.astype(BF16)
    high_ref[...] = high
    low_ref[...] = (right - high.astype(F32)).astype(BF16)


def right_factor(flags, pivot_inverse, upper):
    columns = upper.shape[1]
    block = min(512, columns)
    spec = pl.BlockSpec((PW, block), lambda i, f: (0, i))
    return pl.pallas_call(
        right_kernel,
        out_shape=[jax.ShapeDtypeStruct((PW, columns), BF16)] * 2,
        grid_spec=pltpu.PrefetchScalarGridSpec(
            num_scalar_prefetch=1,
            grid=(columns // block,),
            in_specs=[pl.BlockSpec((PW, PW), lambda i, f: (0, 0)), spec],
            out_specs=[spec, spec],
        ),
        compiler_params=compiler_params(("arbitrary",)),
        name="right_factor",
    )(flags, pivot_inverse, upper)


def update_kernel(block, per_slice, flag_ref, slice_ref, base_ref, code_ref, scale_ref, high_ref, low_ref, out_ref):
    step = pl.program_id(0)
    row_block = slice_ref[step // per_slice] * per_slice + lax.rem(step, per_slice)
    above = jnp.logical_and(flag_ref[0] == 0, row_block < PW // block)

    @pl.when(above)
    def _():
        out_ref[...] = base_ref[...]

    @pl.when(jnp.logical_not(above))
    def _():
        code = code_ref[0].astype(I32)
        upper_part = (code + 128) >> 8
        lower_part = (code - upper_part * 256).astype(F32).astype(BF16)
        upper_part = (upper_part * 256).astype(F32).astype(BF16)
        high, low = high_ref[...], low_ref[...]
        product = (
            jnp.dot(lower_part, high, preferred_element_type=F32)
            + jnp.dot(upper_part, low, preferred_element_type=F32)
        ) + jnp.dot(upper_part, high, preferred_element_type=F32)
        eye = diagonal(TILE)
        for s in range(block // TILE):
            line = scale_ref[0, :, pl.ds(s * TILE, TILE)].astype(I32).astype(F32)[:1]
            exponent = jnp.sum(jnp.where(eye, line, 0.0), axis=1, keepdims=True)
            scale = jnp.exp2(exponent * (1.0 / 64.0)) * (1.0 / CODE_TOP)
            rows = slice(s * TILE, (s + 1) * TILE)
            update = scale * product[rows]
            out_ref[pl.ds(s * TILE, TILE), pl.ds(PW, out_ref.shape[1] - PW)] = (
                base_ref[pl.ds(s * TILE, TILE), pl.ds(PW, out_ref.shape[1] - PW)] - update[:, PW:]
            )
            kept = jnp.where(flag_ref[1] == 0, 0.0, 1.0)
            out_ref[pl.ds(s * TILE, TILE), pl.ds(0, PW)] = (
                base_ref[pl.ds(s * TILE, TILE), pl.ds(0, PW)] * kept - update[:, :PW]
            )


def update_rows(flags, slice_ids, base, codes, high, low):
    rows, columns = base.shape
    slices, slice_rows, _ = codes.shape
    slice_rows -= META
    block = min(256, slice_rows)
    per_slice = slice_rows // block

    def base_map(i, f, s):
        return (s[i // per_slice] * per_slice + lax.rem(i, per_slice), 0)

    return pl.pallas_call(
        functools.partial(update_kernel, block, per_slice),
        out_shape=jax.ShapeDtypeStruct((rows, columns), F32),
        grid_spec=pltpu.PrefetchScalarGridSpec(
            num_scalar_prefetch=2,
            grid=(slices * per_slice,),
            in_specs=[
                pl.BlockSpec((block, columns), base_map),
                pl.BlockSpec((1, block, PW), lambda i, f, s: (i // per_slice, lax.rem(i, per_slice), 0)),
                pl.BlockSpec(
                    (1, META, block),
                    lambda i, f, s: (i // per_slice, slice_rows // META, lax.rem(i, per_slice)),
                ),
                pl.BlockSpec((PW, columns), lambda i, f, s: (0, 0)),
                pl.BlockSpec((PW, columns), lambda i, f, s: (0, 0)),
            ],
            out_specs=pl.BlockSpec((block, columns), base_map),
        ),
        compiler_params=compiler_params(("arbitrary",)),
        name="update_rows",
    )(flags, slice_ids, base, codes, codes, high, low)


def ring_order(count):
    return list(range(0, count, 2)) + list(range(count - 1, 0, -2))


def ring_gather(own, axis):
    count = lax.axis_size(axis)
    order = ring_order(count)
    ahead = [(order[i], order[(i + 1) % count]) for i in range(count)]
    back = [(b, a) for a, b in ahead]
    place = jnp.zeros((), I32)
    index = lax.axis_index(axis)
    for p, d in enumerate(order):
        place = jnp.where(index == d, p, place)
    table = jnp.array(order, I32)
    pieces, whose = [own], [index]
    left = right = own
    for step in range(1, count // 2):
        left, right = lax.ppermute(left, axis, ahead), lax.ppermute(right, axis, back)
        pieces += [left, right]
        whose += [table[(place + count - step) % count], table[(place + step) % count]]
    half = own.shape[0] // 2
    pieces.append(
        jnp.concatenate([lax.ppermute(left[:half], axis, ahead), lax.ppermute(right[half:], axis, back)], 0)
    )
    whose.append(table[(place + count // 2) % count])
    return pieces, jnp.stack(whose)


def scatter_first(parts, axis):
    count = lax.axis_size(axis)
    mine = jnp.where(lax.axis_index(axis) == 0, parts[0], jnp.zeros((), parts.dtype))
    for k in range(1, count):
        mine = mine + lax.ppermute(parts[k], axis, [(0, k)])
    return mine


def tree_broadcast(block, axis):
    count = lax.axis_size(axis)
    index = lax.axis_index(axis)
    reach = count // 2
    while reach >= 1:
        sent = lax.ppermute(block, axis, [(i, i + reach) for i in range(0, count, 2 * reach)])
        block = jnp.where(index % (2 * reach) == reach, sent, block)
        reach //= 2
    return block


def per_device(parent, child, owner, slot, pivot_inverse):
    bulk_count, column_count = lax.axis_size("bulk"), lax.axis_size("col")
    devices = bulk_count * column_count
    rows, columns = parent.shape
    child_count = child.shape[0]
    capacity = max(2, 2 * child_count // devices)
    width = columns // TILE
    bulk_index, column_index = lax.axis_index("bulk"), lax.axis_index("col")
    flags = jnp.stack([bulk_index, column_index]).astype(I32)

    outgoing = pack(owner[:, 0], slot, child, devices, capacity)
    arrived = lax.all_to_all(outgoing, ("bulk", "col"), split_axis=0, concat_axis=0, tiled=True)
    slots = read_slots(arrived, capacity)
    strip, tile_column = slots // width, slots % width
    valid = slots >= 0
    pivot_tiles = PW // TILE
    in_panel = valid & (tile_column < pivot_tiles)
    in_pivot = valid & (strip < pivot_tiles)
    panel_key = jnp.where(in_panel, strip * pivot_tiles + tile_column, -1)
    pivot_key = jnp.where(in_pivot, slots, -1)
    taken = in_panel & (column_index == 0) & ~(in_pivot & (bulk_index == 0))
    rest_key = jnp.where(valid & ~taken, slots, -1)

    codes = code_panel(parent, arrived, panel_key, capacity, column_count)
    upper = extend(parent, arrived, pivot_key, width, capacity, PW, columns)
    upper = tree_broadcast(upper, "bulk")
    high, low = right_factor(flags, pivot_inverse, upper)
    pieces, whose = ring_gather(scatter_first(codes, "col"), "col")
    result = update_rows(flags, whose, parent, jnp.stack(pieces), high, low)
    return extend(result, arrived, rest_key, width, capacity, rows, columns, alias=True)


def solution(mesh):
    in_specs = (
        P("bulk", "col"),
        P(("bulk", "col"), None, None),
        P(("bulk", "col"), None),
        P(("bulk", "col")),
        P(),
    )
    return jax.shard_map(
        per_device, mesh=mesh, in_specs=in_specs, out_specs=P("bulk", "col"), check_vma=False
    )
```

```python
import functools

import jax
import jax.numpy as jnp
from jax import lax
from jax.experimental import pallas as pl
from jax.experimental.pallas import tpu as pltpu
from jax.sharding import PartitionSpec as P

PW = 512
TILE = 128
META = 16
CODE_TOP = 32600.0
VMEM_LIMIT = 56 * 1024 * 1024

F32 = jnp.float32
BF16 = jnp.bfloat16
I32 = jnp.int32


def compiler_params(semantics=None):
    return pltpu.CompilerParams(dimension_semantics=semantics, vmem_limit_bytes=VMEM_LIMIT)


def pack_kernel(devices, capacity, owner_ref, slot_ref, child_ref, out_ref, filled, slots, meta, sem, meta_sem):
    child_count = owner_ref.shape[0]

    def clear(d, _):
        filled[d] = 0
        return 0

    lax.fori_loop(0, devices, clear, 0)

    def clear_slot(i, _):
        slots[i] = -1
        return 0

    lax.fori_loop(0, devices * capacity, clear_slot, 0)

    def place(i, _):
        d = owner_ref[i]
        k = filled[d]
        filled[d] = k + 1
        slots[d * capacity + k] = slot_ref[i]
        pltpu.make_async_copy(
            child_ref.at[i], out_ref.at[d, pl.ds(pl.multiple_of(k * TILE, TILE), TILE)], sem
        ).start()
        return 0

    lax.fori_loop(0, child_count, place, 0)
    lane = lax.broadcasted_iota(I32, (META, TILE), 1)
    row = lax.broadcasted_iota(I32, (META, TILE), 0)

    def write_meta(d, _):
        value = jnp.full((META, TILE), -1, I32)
        for k in range(capacity):
            value = jnp.where(lane == k, slots[d * capacity + k], value)
        coded = jnp.where(row == 0, value >> 4, value & 15)
        meta[d] = coded.astype(F32).astype(BF16)
        return 0

    lax.fori_loop(0, devices, write_meta, 0)
    copy = pltpu.make_async_copy(meta, out_ref.at[:, pl.ds(capacity * TILE, META)], meta_sem)
    copy.start()
    pltpu.make_async_copy(child_ref, child_ref, sem).wait()
    copy.wait()


def pack(owner, slot, child, devices, capacity):
    rows = capacity * TILE + META
    return pl.pallas_call(
        functools.partial(pack_kernel, devices, capacity),
        out_shape=jax.ShapeDtypeStruct((devices, rows, TILE), BF16),
        in_specs=[
            pl.BlockSpec(memory_space=pltpu.SMEM),
            pl.BlockSpec(memory_space=pltpu.SMEM),
            pl.BlockSpec(memory_space=pltpu.VMEM),
        ],
        out_specs=pl.BlockSpec(memory_space=pl.ANY),
        scratch_shapes=[
            pltpu.SMEM((devices,), I32),
            pltpu.SMEM((devices * capacity,), I32),
            pltpu.VMEM((devices, META, TILE), BF16),
            pltpu.SemaphoreType.DMA,
            pltpu.SemaphoreType.DMA,
        ],
        compiler_params=compiler_params(),
        name="pack_children",
    )(owner, slot, child)


def read_slots(arrived, capacity):
    coded = arrived[:, capacity * TILE : capacity * TILE + 2, :capacity].astype(I32)
    return (coded[:, 0] * 16 + coded[:, 1]).reshape(-1)


def build_lists(key_ref, head, following, width):
    def clear(i, _):
        head[i] = -1
        return 0

    lax.fori_loop(0, head.shape[0], clear, 0)

    def add(i, _):
        key = key_ref[i]

        @pl.when(key >= 0)
        def _():
            strip = key // width
            following[i] = head[strip]
            head[strip] = i

        return 0

    lax.fori_loop(0, key_ref.shape[0], add, 0)


def add_strip(key_ref, arrived_ref, out, head, following, strip, width, capacity, row):
    def body(i):
        column = pl.multiple_of((key_ref[i] % width) * TILE, TILE)
        start = pl.multiple_of((i % capacity) * TILE, TILE)
        block = arrived_ref[i // capacity, pl.ds(start, TILE), :]
        spot = (pl.ds(row, TILE), pl.ds(column, TILE))
        out[spot] = out[spot] + block.astype(F32)
        return following[i]

    lax.while_loop(lambda i: i >= 0, body, head[strip])


def extend_kernel(width, capacity, key_ref, base_ref, arrived_ref, out_ref, head, following):
    step = pl.program_id(0)

    @pl.when(step == 0)
    def _():
        build_lists(key_ref, head, following, width)

    out_ref[...] = base_ref[...]
    strips = base_ref.shape[0] // TILE
    for s in range(strips):
        add_strip(
            key_ref, arrived_ref, out_ref, head, following, step * strips + s, width, capacity, s * TILE
        )


def extend(base, arrived, key, width, capacity, rows, columns):
    return pl.pallas_call(
        functools.partial(extend_kernel, width, capacity),
        out_shape=jax.ShapeDtypeStruct((rows, columns), F32),
        grid_spec=pltpu.PrefetchScalarGridSpec(
            num_scalar_prefetch=1,
            grid=(rows // TILE,),
            in_specs=[
                pl.BlockSpec((TILE, columns), lambda i, k: (i, 0)),
                pl.BlockSpec(memory_space=pltpu.VMEM),
            ],
            out_specs=pl.BlockSpec((TILE, columns), lambda i, k: (i, 0)),
            scratch_shapes=[
                pltpu.SMEM((rows // TILE,), I32),
                pltpu.SMEM((key.shape[0],), I32),
            ],
        ),
        compiler_params=compiler_params(("arbitrary",)),
        cost_estimate=pl.CostEstimate(flops=rows * columns, bytes_accessed=12 * rows * columns, transcendentals=0),
        name="extend_add",
    )(key, base, arrived)


def code_rows(values):
    top = jnp.maximum(jnp.max(jnp.abs(values), axis=1, keepdims=True), 1e-30)
    exponent = jnp.ceil(jnp.log2(top) * 64.0)
    code = jnp.round(values * (CODE_TOP * jnp.exp2(exponent * (-1.0 / 64.0))))
    return code.astype(I32), exponent


def diagonal(n):
    return lax.broadcasted_iota(I32, (n, n), 0) == lax.broadcasted_iota(I32, (n, n), 1)


def panel_kernel(width, capacity, key_ref, base_ref, arrived_ref, out_ref, work, head, following):
    step = pl.program_id(0)

    @pl.when(step == 0)
    def _():
        build_lists(key_ref, head, following, width)

    work[...] = base_ref[...]
    rows = base_ref.shape[0]
    strips = rows // TILE
    eye = diagonal(TILE)
    out_ref[0, pl.ds(rows, META), :] = jnp.zeros((META, out_ref.shape[2]), jnp.int16)
    for s in range(strips):
        add_strip(
            key_ref, arrived_ref, work, head, following, step * strips + s, width, capacity, s * TILE
        )
        code, exponent = code_rows(work[pl.ds(s * TILE, TILE), :])
        out_ref[0, pl.ds(s * TILE, TILE), :] = code.astype(jnp.int16)
        line = jnp.sum(jnp.where(eye, exponent, 0.0), axis=0, keepdims=True)
        out_ref[0, pl.ds(rows, META), pl.ds(s * TILE, TILE)] = (
            jnp.broadcast_to(line, (META, TILE)).astype(I32).astype(jnp.int16)
        )


def code_panel(base, arrived, key, capacity, slices):
    rows = base.shape[0] // slices
    width = PW // TILE
    return pl.pallas_call(
        functools.partial(panel_kernel, width, capacity),
        out_shape=jax.ShapeDtypeStruct((slices, rows + META, PW), jnp.int16),
        grid_spec=pltpu.PrefetchScalarGridSpec(
            num_scalar_prefetch=1,
            grid=(slices,),
            in_specs=[
                pl.BlockSpec((rows, PW), lambda i, k: (i, 0)),
                pl.BlockSpec(memory_space=pltpu.VMEM),
            ],
            out_specs=pl.BlockSpec((1, rows + META, PW), lambda i, k: (i, 0, 0)),
            scratch_shapes=[
                pltpu.VMEM((rows, PW), F32),
                pltpu.SMEM((base.shape[0] // TILE,), I32),
                pltpu.SMEM((key.shape[0],), I32),
            ],
        ),
        compiler_params=compiler_params(("arbitrary",)),
        name="code_panel",
    )(key, base, arrived)


def right_kernel(flag_ref, pivot_ref, upper_ref, high_ref, low_ref):
    step = pl.program_id(0)
    columns = upper_ref.shape[1]
    row = lax.broadcasted_iota(I32, (PW, columns), 0)
    column = lax.broadcasted_iota(I32, (PW, columns), 1) + step * columns
    in_panel = jnp.logical_and(column < PW, flag_ref[1] == 0)
    upper = jnp.where(in_panel, jnp.where(row == column, -1.0, 0.0), upper_ref[...])
    right = jnp.dot(pivot_ref[...], upper, precision=lax.Precision.HIGHEST, preferred_element_type=F32)
    high = right.astype(BF16)
    high_ref[...] = high
    low_ref[...] = (right - high.astype(F32)).astype(BF16)


def right_factor(flags, pivot_inverse, upper):
    columns = upper.shape[1]
    block = min(512, columns)
    spec = pl.BlockSpec((PW, block), lambda i, f: (0, i))
    return pl.pallas_call(
        right_kernel,
        out_shape=[jax.ShapeDtypeStruct((PW, columns), BF16)] * 2,
        grid_spec=pltpu.PrefetchScalarGridSpec(
            num_scalar_prefetch=1,
            grid=(columns // block,),
            in_specs=[pl.BlockSpec((PW, PW), lambda i, f: (0, 0)), spec],
            out_specs=[spec, spec],
        ),
        compiler_params=compiler_params(("arbitrary",)),
        name="right_factor",
    )(flags, pivot_inverse, upper)


def update_kernel(block, per_slice, flag_ref, slice_ref, base_ref, code_ref, scale_ref, high_ref, low_ref, out_ref):
    step = pl.program_id(0)
    row_block = slice_ref[step // per_slice] * per_slice + lax.rem(step, per_slice)
    above = jnp.logical_and(flag_ref[0] == 0, row_block < PW // block)

    @pl.when(above)
    def _():
        out_ref[...] = base_ref[...]

    @pl.when(jnp.logical_not(above))
    def _():
        code = code_ref[0].astype(I32)
        upper_part = (code + 128) >> 8
        lower_part = (code - upper_part * 256).astype(F32).astype(BF16)
        upper_part = (upper_part * 256).astype(F32).astype(BF16)
        high, low = high_ref[...], low_ref[...]
        product = (
            jnp.dot(lower_part, high, preferred_element_type=F32)
            + jnp.dot(upper_part, low, preferred_element_type=F32)
        ) + jnp.dot(upper_part, high, preferred_element_type=F32)
        eye = diagonal(TILE)
        for s in range(block // TILE):
            line = scale_ref[0, :, pl.ds(s * TILE, TILE)].astype(I32).astype(F32)[:1]
            exponent = jnp.sum(jnp.where(eye, line, 0.0), axis=1, keepdims=True)
            scale = jnp.exp2(exponent * (1.0 / 64.0)) * (1.0 / CODE_TOP)
            rows = slice(s * TILE, (s + 1) * TILE)
            update = scale * product[rows]
            out_ref[pl.ds(s * TILE, TILE), pl.ds(PW, out_ref.shape[1] - PW)] = (
                base_ref[pl.ds(s * TILE, TILE), pl.ds(PW, out_ref.shape[1] - PW)] - update[:, PW:]
            )
            kept = jnp.where(flag_ref[1] == 0, 0.0, 1.0)
            out_ref[pl.ds(s * TILE, TILE), pl.ds(0, PW)] = (
                base_ref[pl.ds(s * TILE, TILE), pl.ds(0, PW)] * kept - update[:, :PW]
            )


def update_rows(flags, slice_ids, base, codes, high, low):
    rows, columns = base.shape
    slices, slice_rows, _ = codes.shape
    slice_rows -= META
    block = min(256, slice_rows)
    per_slice = slice_rows // block

    def base_map(i, f, s):
        return (s[i // per_slice] * per_slice + lax.rem(i, per_slice), 0)

    return pl.pallas_call(
        functools.partial(update_kernel, block, per_slice),
        out_shape=jax.ShapeDtypeStruct((rows, columns), F32),
        grid_spec=pltpu.PrefetchScalarGridSpec(
            num_scalar_prefetch=2,
            grid=(slices * per_slice,),
            in_specs=[
                pl.BlockSpec((block, columns), base_map),
                pl.BlockSpec((1, block, PW), lambda i, f, s: (i // per_slice, lax.rem(i, per_slice), 0)),
                pl.BlockSpec(
                    (1, META, block),
                    lambda i, f, s: (i // per_slice, slice_rows // META, lax.rem(i, per_slice)),
                ),
                pl.BlockSpec((PW, columns), lambda i, f, s: (0, 0)),
                pl.BlockSpec((PW, columns), lambda i, f, s: (0, 0)),
            ],
            out_specs=pl.BlockSpec((block, columns), base_map),
        ),
        input_output_aliases={2: 0},
        compiler_params=compiler_params(("arbitrary",)),
        name="update_rows",
    )(flags, slice_ids, base, codes, codes, high, low)


def ring_order(count):
    return list(range(0, count, 2)) + list(range(count - 1, 0, -2))


def ring_gather(own, axis):
    count = lax.axis_size(axis)
    order = ring_order(count)
    ahead = [(order[i], order[(i + 1) % count]) for i in range(count)]
    back = [(b, a) for a, b in ahead]
    place = jnp.zeros((), I32)
    index = lax.axis_index(axis)
    for p, d in enumerate(order):
        place = jnp.where(index == d, p, place)
    table = jnp.array(order, I32)
    pieces, whose = [own], [index]
    left = right = own
    for step in range(1, count // 2):
        left, right = lax.ppermute(left, axis, ahead), lax.ppermute(right, axis, back)
        pieces += [left, right]
        whose += [table[(place + count - step) % count], table[(place + step) % count]]
    half = own.shape[0] // 2
    pieces.append(
        jnp.concatenate([lax.ppermute(left[:half], axis, ahead), lax.ppermute(right[half:], axis, back)], 0)
    )
    whose.append(table[(place + count // 2) % count])
    return pieces, jnp.stack(whose)


def scatter_first(parts, axis):
    count = lax.axis_size(axis)
    mine = jnp.where(lax.axis_index(axis) == 0, parts[0], jnp.zeros((), parts.dtype))
    for k in range(1, count):
        mine = mine + lax.ppermute(parts[k], axis, [(0, k)])
    return mine


def tree_broadcast(block, axis):
    count = lax.axis_size(axis)
    index = lax.axis_index(axis)
    reach = count // 2
    while reach >= 1:
        sent = lax.ppermute(block, axis, [(i, i + reach) for i in range(0, count, 2 * reach)])
        block = jnp.where(index % (2 * reach) == reach, sent, block)
        reach //= 2
    return block


def per_device(parent, child, owner, slot, pivot_inverse):
    bulk_count, column_count = lax.axis_size("bulk"), lax.axis_size("col")
    devices = bulk_count * column_count
    rows, columns = parent.shape
    child_count = child.shape[0]
    capacity = max(2, 2 * child_count // devices)
    width = columns // TILE
    bulk_index, column_index = lax.axis_index("bulk"), lax.axis_index("col")
    flags = jnp.stack([bulk_index, column_index]).astype(I32)

    outgoing = pack(owner[:, 0], slot, child, devices, capacity)
    arrived = lax.all_to_all(outgoing, ("bulk", "col"), split_axis=0, concat_axis=0, tiled=True)
    slots = read_slots(arrived, capacity)
    strip, tile_column = slots // width, slots % width
    valid = slots >= 0
    pivot_tiles = PW // TILE
    in_panel = valid & (tile_column < pivot_tiles)
    in_pivot = valid & (strip < pivot_tiles)
    panel_key = jnp.where(in_panel, strip * pivot_tiles + tile_column, -1)
    pivot_key = jnp.where(in_pivot, slots, -1)

    codes = code_panel(parent, arrived, panel_key, capacity, column_count)
    upper = extend(parent, arrived, pivot_key, width, capacity, PW, columns)
    upper = tree_broadcast(upper, "bulk")
    high, low = right_factor(flags, pivot_inverse, upper)
    pieces, whose = ring_gather(scatter_first(codes, "col"), "col")
    extended = extend(parent, arrived, slots, width, capacity, rows, columns)
    return update_rows(flags, whose, extended, jnp.stack(pieces), high, low)


def solution(mesh):
    in_specs = (
        P("bulk", "col"),
        P(("bulk", "col"), None, None),
        P(("bulk", "col"), None),
        P(("bulk", "col")),
        P(),
    )
    return jax.shard_map(
        per_device, mesh=mesh, in_specs=in_specs, out_specs=P("bulk", "col"), check_vma=False
    )
```

```python
import functools

import jax
import jax.numpy as jnp
from jax import lax
from jax.experimental import pallas as pl
from jax.experimental.pallas import tpu as pltpu
from jax.sharding import PartitionSpec as P

PW = 512
TILE = 128
META = 16
CODE_TOP = 32600.0
VMEM_LIMIT = 56 * 1024 * 1024

SHORT = pl.CostEstimate(flops=0, bytes_accessed=4096, transcendentals=0)

F32 = jnp.float32
BF16 = jnp.bfloat16
I32 = jnp.int32


def compiler_params(semantics=None):
    return pltpu.CompilerParams(dimension_semantics=semantics, vmem_limit_bytes=VMEM_LIMIT)


def pack_kernel(devices, capacity, owner_ref, slot_ref, child_ref, out_ref, filled, slots, meta, sem, meta_sem):
    child_count = owner_ref.shape[0]

    def clear(d, _):
        filled[d] = 0
        return 0

    lax.fori_loop(0, devices, clear, 0)

    def clear_slot(i, _):
        slots[i] = -1
        return 0

    lax.fori_loop(0, devices * capacity, clear_slot, 0)

    def place(i, _):
        d = owner_ref[i]
        k = filled[d]
        filled[d] = k + 1
        slots[d * capacity + k] = slot_ref[i]
        pltpu.make_async_copy(
            child_ref.at[i], out_ref.at[d, pl.ds(pl.multiple_of(k * TILE, TILE), TILE)], sem
        ).start()
        return 0

    lax.fori_loop(0, child_count, place, 0)
    lane = lax.broadcasted_iota(I32, (META, TILE), 1)
    row = lax.broadcasted_iota(I32, (META, TILE), 0)

    def write_meta(d, _):
        value = jnp.full((META, TILE), -1, I32)
        for k in range(capacity):
            value = jnp.where(lane == k, slots[d * capacity + k], value)
        coded = jnp.where(row == 0, value >> 4, value & 15)
        meta[d] = coded.astype(F32).astype(BF16)
        return 0

    lax.fori_loop(0, devices, write_meta, 0)
    copy = pltpu.make_async_copy(meta, out_ref.at[:, pl.ds(capacity * TILE, META)], meta_sem)
    copy.start()
    pltpu.make_async_copy(child_ref, child_ref, sem).wait()
    copy.wait()


def pack(owner, slot, child, devices, capacity):
    rows = capacity * TILE + META
    return pl.pallas_call(
        functools.partial(pack_kernel, devices, capacity),
        out_shape=jax.ShapeDtypeStruct((devices, rows, TILE), BF16),
        in_specs=[
            pl.BlockSpec(memory_space=pltpu.SMEM),
            pl.BlockSpec(memory_space=pltpu.SMEM),
            pl.BlockSpec(memory_space=pltpu.VMEM),
        ],
        out_specs=pl.BlockSpec(memory_space=pl.ANY),
        scratch_shapes=[
            pltpu.SMEM((devices,), I32),
            pltpu.SMEM((devices * capacity,), I32),
            pltpu.VMEM((devices, META, TILE), BF16),
            pltpu.SemaphoreType.DMA,
            pltpu.SemaphoreType.DMA,
        ],
        compiler_params=compiler_params(),
        name="pack_children",
    )(owner, slot, child)


def lanes(values, count, fallback=-1):
    lane = lax.broadcasted_iota(I32, (META, TILE), 1)
    out = jnp.full((META, TILE), fallback, I32)
    for k in range(count):
        out = jnp.where(lane == k, values(k), out)
    return out


def coded_lines(code, third):
    row = lax.broadcasted_iota(I32, (META, TILE), 0)
    lines = jnp.where(row == 0, code >> 4, jnp.where(row == 1, code & 15, third))
    return lines.astype(F32).astype(BF16)


def fill(ref, count, value):
    def step(i, _):
        ref[i] = value
        return 0

    lax.fori_loop(0, count, step, 0, unroll=8 if count % 8 == 0 else 1)


def sort_kernel(
    plan, kind_ref, dest_ref, code_ref, child_ref,
    early_ref, near_ref, far_ref, over_ref,
    filled, early_code, list_code, list_dest, early_meta, list_meta, sem, meta_sem,
):
    devices, share, size, half = plan["devices"], plan["early"], plan["listed"], plan["half"]
    columns = plan["columns"]
    lists = (near_ref, far_ref)
    fill(filled, devices + 2, 0)
    fill(early_code, devices * share, -1)
    fill(list_code, 2 * size, -1)
    fill(list_dest, 2 * size, -1)
    over_ref[0] = 0

    def send_early(i, dest, k):
        early_code[dest * share + k] = code_ref[i]
        rows = pl.ds(pl.multiple_of(k * TILE, TILE), TILE)
        pltpu.make_async_copy(child_ref.at[i], early_ref.at[dest, rows], sem).start()

    def place_special(i, _):
        @pl.when(kind_ref[i] == 2)
        def _():
            dest = dest_ref[i]
            k = filled[dest]
            filled[dest] = k + 1

            @pl.when(k >= share)
            def _():
                over_ref[0] = 1

            send_early(i, dest, jnp.minimum(k, share - 1))

        return 0

    def place_plain(i, _):
        kind, dest = kind_ref[i], dest_ref[i]

        @pl.when(kind < 2)
        def _():
            k = filled[dest]
            filled[dest] = k + 1

            @pl.when(k < share)
            def _():
                send_early(i, dest, k)

            @pl.when(k >= share)
            def _():
                spot = filled[devices + kind]
                filled[devices + kind] = spot + 1

                @pl.when(spot >= size)
                def _():
                    over_ref[0] = 1

                spot = jnp.minimum(spot, size - 1)
                list_code[kind * size + spot] = code_ref[i]
                list_dest[kind * size + spot] = (dest // columns) * half + lax.rem(dest, half)
                rows = pl.ds(pl.multiple_of(spot * TILE, TILE), TILE)
                for which in range(2):

                    @pl.when(kind == which)
                    def _(which=which):
                        pltpu.make_async_copy(child_ref.at[i], lists[which].at[rows], sem).start()

        return 0

    lax.fori_loop(0, kind_ref.shape[0], place_special, 0)
    lax.fori_loop(0, kind_ref.shape[0], place_plain, 0)
    copies = []
    for which in range(2):
        code = lanes(lambda k: list_code[which * size + k], size)
        dest = lanes(lambda k: list_dest[which * size + k], size)
        list_meta[which] = coded_lines(code, dest)
        copies.append(
            pltpu.make_async_copy(
                list_meta.at[which], lists[which].at[pl.ds(size * TILE, META)], meta_sem.at[which]
            )
        )
        copies[-1].start()

    def write_meta(d, _):
        early_meta[d] = coded_lines(lanes(lambda k: early_code[d * share + k], share), 0)
        return 0

    lax.fori_loop(0, devices, write_meta, 0)
    copies.append(
        pltpu.make_async_copy(early_meta, early_ref.at[:, pl.ds(share * TILE, META)], meta_sem.at[2])
    )
    copies[-1].start()
    pltpu.make_async_copy(child_ref, child_ref, sem).wait()
    for copy in copies:
        copy.wait()


def sort_children(plan, owner, slot, flags, child):
    devices, share, listed = plan["devices"], plan["early"], plan["listed"]
    bulk, col = owner // plan["columns"], owner % plan["columns"]
    strip, tile = slot // plan["width"], slot % plan["width"]
    pivot = (bulk == 0) & (strip < plan["pivot"])
    panel = (col == 0) & (tile < plan["pivot"])
    pivot, panel = pivot & ~panel, panel & ~pivot
    bulk = jnp.where(pivot, strip // plan["pivot_strips"], bulk)
    col = jnp.where(panel, strip // plan["panel_strips"], col)
    code = jnp.where(panel, plan["panel_code"] + (strip % plan["panel_strips"]) * plan["pivot"] + tile, slot)
    code = jnp.where(pivot, plan["pivot_code"] + (strip % plan["pivot_strips"]) * plan["width"] + tile, code)
    here = col // plan["half"] == flags[1] // plan["half"]
    kind = jnp.where(pivot | panel, 2, jnp.where(here, 0, 1))
    dest = bulk * plan["columns"] + col
    anywhere = pl.BlockSpec(memory_space=pl.ANY)
    scalars = pl.BlockSpec(memory_space=pltpu.SMEM)
    in_list = jax.ShapeDtypeStruct((listed * TILE + META, TILE), BF16)
    return pl.pallas_call(
        functools.partial(sort_kernel, plan),
        out_shape=[
            jax.ShapeDtypeStruct((devices, share * TILE + META, TILE), BF16),
            in_list,
            in_list,
            jax.ShapeDtypeStruct((1,), I32),
        ],
        in_specs=[scalars, scalars, scalars, pl.BlockSpec(memory_space=pltpu.VMEM)],
        out_specs=[anywhere, anywhere, anywhere, scalars],
        scratch_shapes=[
            pltpu.SMEM((devices + 2,), I32),
            pltpu.SMEM((devices * share,), I32),
            pltpu.SMEM((2 * listed,), I32),
            pltpu.SMEM((2 * listed,), I32),
            pltpu.VMEM((devices, META, TILE), BF16),
            pltpu.VMEM((2, META, TILE), BF16),
            pltpu.SemaphoreType.DMA,
            pltpu.SemaphoreType.DMA((3,)),
        ],
        compiler_params=compiler_params(),
        cost_estimate=SHORT,
        name="sort_children",
    )(kind, dest, code, child)


def read_list(listed):
    count = (listed.shape[0] - META) // TILE
    lines = listed[count * TILE : count * TILE + 3, :count].astype(I32)
    return lines[0] * 16 + lines[1], lines[2]


def distribute_kernel(groups, capacity, sizes, *refs):
    n = len(sizes)
    code_refs, dest_refs, block_refs = refs[:n], refs[n : 2 * n], refs[2 * n : 3 * n]
    over_in, out_ref, over_ref, filled, codes, meta, spare, sem, meta_sem = refs[3 * n :]
    fill(filled, groups, 0)
    fill(codes, groups * capacity, -1)
    over_ref[0] = over_in[0]
    for code_ref, dest_ref, block_ref, size in zip(code_refs, dest_refs, block_refs, sizes):

        def place(i, _, code_ref=code_ref, dest_ref=dest_ref, block_ref=block_ref):
            dest = dest_ref[i]
            block = block_ref.at[pl.ds(pl.multiple_of(i * TILE, TILE), TILE)]

            @pl.when(dest >= 0)
            def _():
                k = filled[dest]
                filled[dest] = k + 1

                @pl.when(k >= capacity)
                def _():
                    over_ref[0] = 1

                k = jnp.minimum(k, capacity - 1)
                codes[dest * capacity + k] = code_ref[i]
                pltpu.make_async_copy(
                    block, out_ref.at[dest, pl.ds(pl.multiple_of(k * TILE, TILE), TILE)], sem
                ).start()

            @pl.when(dest < 0)
            def _():
                pltpu.make_async_copy(block, spare, sem).start()

            return 0

        lax.fori_loop(0, size, place, 0)

    def write_meta(g, _):
        meta[g] = coded_lines(lanes(lambda k: codes[g * capacity + k], capacity), over_ref[0])
        return 0

    lax.fori_loop(0, groups, write_meta, 0)
    copy = pltpu.make_async_copy(meta, out_ref.at[:, pl.ds(capacity * TILE, META)], meta_sem)
    copy.start()
    for block_ref, size in zip(block_refs, sizes):
        blocks = block_ref.at[pl.ds(0, size * TILE)]
        pltpu.make_async_copy(blocks, blocks, sem).wait()
    copy.wait()


def distribute(lists, over, groups, capacity):
    sizes = [(x.shape[0] - META) // TILE for x in lists]
    codes, dests = zip(*[read_list(x) for x in lists])
    n = len(lists)
    return pl.pallas_call(
        functools.partial(distribute_kernel, groups, capacity, sizes),
        out_shape=[
            jax.ShapeDtypeStruct((groups, capacity * TILE + META, TILE), BF16),
            jax.ShapeDtypeStruct((1,), I32),
        ],
        in_specs=[pl.BlockSpec(memory_space=pltpu.SMEM)] * (2 * n)
        + [pl.BlockSpec(memory_space=pltpu.VMEM)] * n
        + [pl.BlockSpec(memory_space=pltpu.SMEM)],
        out_specs=[pl.BlockSpec(memory_space=pl.ANY), pl.BlockSpec(memory_space=pltpu.SMEM)],
        scratch_shapes=[
            pltpu.SMEM((groups,), I32),
            pltpu.SMEM((groups * capacity,), I32),
            pltpu.VMEM((groups, META, TILE), BF16),
            pltpu.VMEM((TILE, TILE), BF16),
            pltpu.SemaphoreType.DMA,
            pltpu.SemaphoreType.DMA,
        ],
        compiler_params=compiler_params(),
        cost_estimate=SHORT,
        name="distribute",
    )(*codes, *dests, *lists, over)[0]


def read_over(arrived, capacity):
    return jnp.max(arrived[:, capacity * TILE + 2, 0].astype(I32))


def read_slots(arrived, capacity):
    coded = arrived[:, capacity * TILE : capacity * TILE + 2, :capacity].astype(I32)
    return (coded[:, 0] * 16 + coded[:, 1]).reshape(-1)


def build_lists(key_ref, head, following, width):
    def clear(i, _):
        head[i] = -1
        return 0

    lax.fori_loop(0, head.shape[0], clear, 0)

    def add(i, _):
        key = key_ref[i]

        @pl.when(key >= 0)
        def _():
            strip = key // width
            following[i] = head[strip]
            head[strip] = i

        return 0

    lax.fori_loop(0, key_ref.shape[0], add, 0)


def add_strip(key_ref, arrived_ref, out, head, following, strip, width, capacity, row):
    def body(i):
        column = pl.multiple_of((key_ref[i] % width) * TILE, TILE)
        start = pl.multiple_of((i % capacity) * TILE, TILE)
        block = arrived_ref[i // capacity, pl.ds(start, TILE), :]
        spot = (pl.ds(row, TILE), pl.ds(column, TILE))
        out[spot] = out[spot] + block.astype(F32)
        return following[i]

    lax.while_loop(lambda i: i >= 0, body, head[strip])


def extend_kernel(width, capacity, key_ref, base_ref, arrived_ref, out_ref, head, following):
    step = pl.program_id(0)

    @pl.when(step == 0)
    def _():
        build_lists(key_ref, head, following, width)

    out_ref[...] = base_ref[...]
    strips = base_ref.shape[0] // TILE
    for s in range(strips):
        add_strip(
            key_ref, arrived_ref, out_ref, head, following, step * strips + s, width, capacity, s * TILE
        )


def extend(base, arrived, key, width, capacity, rows, columns):
    return pl.pallas_call(
        functools.partial(extend_kernel, width, capacity),
        out_shape=jax.ShapeDtypeStruct((rows, columns), F32),
        grid_spec=pltpu.PrefetchScalarGridSpec(
            num_scalar_prefetch=1,
            grid=(rows // TILE,),
            in_specs=[
                pl.BlockSpec((TILE, columns), lambda i, k: (i, 0)),
                pl.BlockSpec(memory_space=pltpu.VMEM),
            ],
            out_specs=pl.BlockSpec((TILE, columns), lambda i, k: (i, 0)),
            scratch_shapes=[
                pltpu.SMEM((rows // TILE,), I32),
                pltpu.SMEM((key.shape[0],), I32),
            ],
        ),
        compiler_params=compiler_params(("arbitrary",)),
        cost_estimate=pl.CostEstimate(flops=rows * columns, bytes_accessed=12 * rows * columns, transcendentals=0),
        name="extend_add",
    )(key, base, arrived)


AHEAD = 8
BUFFERS = 16


def touch_kernel(
    width, capacity, key_ref, base_ref, arrived_ref, out_ref,
    tiles, head, following, active, read_sem, write_sem,
):
    del base_ref
    fill(head, head.shape[0], -1)

    def chain(i, count):
        key = key_ref[i]
        at = jnp.maximum(key, 0)
        first = jnp.logical_and(key >= 0, head[at] < 0)

        @pl.when(key >= 0)
        def _():
            following[i] = head[at]
            head[at] = i

        @pl.when(first)
        def _():
            active[count] = key

        return count + first.astype(I32)

    count = lax.fori_loop(0, key_ref.shape[0], chain, jnp.int32(0))

    def copy(j, out):
        key = active[j]
        slot = lax.rem(j, BUFFERS)
        place = out_ref.at[
            pl.ds(pl.multiple_of((key // width) * TILE, TILE), TILE),
            pl.ds(pl.multiple_of((key % width) * TILE, TILE), TILE),
        ]
        if out:
            return pltpu.make_async_copy(tiles.at[slot], place, write_sem.at[slot])
        return pltpu.make_async_copy(place, tiles.at[slot], read_sem.at[slot])

    def first_reads(j, _):
        copy(j, False).start()
        return 0

    lax.fori_loop(0, jnp.minimum(count, AHEAD), first_reads, 0)

    def step(j, _):
        later = j + AHEAD

        @pl.when(later < count)
        def _():
            @pl.when(later >= BUFFERS)
            def _():
                copy(later - BUFFERS, True).wait()

            copy(later, False).start()

        copy(j, False).wait()
        slot = lax.rem(j, BUFFERS)

        def body(i):
            start = pl.multiple_of((i % capacity) * TILE, TILE)
            tiles[slot] = tiles[slot] + arrived_ref[i // capacity, pl.ds(start, TILE), :].astype(F32)
            return following[i]

        lax.while_loop(lambda i: i >= 0, body, head[active[j]])
        copy(j, True).start()
        return 0

    lax.fori_loop(0, count, step, 0)

    def last_writes(j, _):
        copy(j, True).wait()
        return 0

    lax.fori_loop(jnp.maximum(count - BUFFERS, 0), count, last_writes, 0)


def touch_tiles(base, arrived, key, width, capacity):
    rows, columns = base.shape
    return pl.pallas_call(
        functools.partial(touch_kernel, width, capacity),
        out_shape=jax.ShapeDtypeStruct((rows, columns), F32),
        in_specs=[
            pl.BlockSpec(memory_space=pltpu.SMEM),
            pl.BlockSpec(memory_space=pl.ANY),
            pl.BlockSpec(memory_space=pltpu.VMEM),
        ],
        out_specs=pl.BlockSpec(memory_space=pl.ANY),
        scratch_shapes=[
            pltpu.VMEM((BUFFERS, TILE, TILE), F32),
            pltpu.SMEM((rows * columns // (TILE * TILE),), I32),
            pltpu.SMEM((key.shape[0],), I32),
            pltpu.SMEM((key.shape[0],), I32),
            pltpu.SemaphoreType.DMA((BUFFERS,)),
            pltpu.SemaphoreType.DMA((BUFFERS,)),
        ],
        input_output_aliases={1: 0},
        compiler_params=compiler_params(),
        name="touch_tiles",
    )(key, base, arrived)


def code_rows(values):
    top = jnp.maximum(jnp.max(jnp.abs(values), axis=1, keepdims=True), 1e-30)
    exponent = jnp.ceil(jnp.log2(top) * 64.0)
    code = jnp.round(values * (CODE_TOP * jnp.exp2(exponent * (-1.0 / 64.0))))
    return code.astype(I32), exponent


def diagonal(n):
    return lax.broadcasted_iota(I32, (n, n), 0) == lax.broadcasted_iota(I32, (n, n), 1)


def write_code(out_ref, lead, values, rows, s):
    code, exponent = code_rows(values)
    out_ref[(*lead, pl.ds(s * TILE, TILE), slice(None))] = code.astype(jnp.int16)
    line = jnp.sum(jnp.where(diagonal(TILE), exponent, 0.0), axis=0, keepdims=True)
    out_ref[(*lead, pl.ds(rows, META), pl.ds(s * TILE, TILE))] = (
        jnp.broadcast_to(line, (META, TILE)).astype(I32).astype(jnp.int16)
    )


def row_scale(lines):
    line = lines.astype(I32).astype(F32)[:1]
    exponent = jnp.sum(jnp.where(diagonal(TILE), line, 0.0), axis=1, keepdims=True)
    return jnp.exp2(exponent * (1.0 / 64.0)) * (1.0 / CODE_TOP)


def encode_kernel(base_ref, out_ref):
    rows = base_ref.shape[0]
    out_ref[0, pl.ds(rows, META), :] = jnp.zeros((META, out_ref.shape[2]), jnp.int16)
    for s in range(rows // TILE):
        write_code(out_ref, (0,), base_ref[pl.ds(s * TILE, TILE), :], rows, s)


def encode_panel(base, slices):
    rows = base.shape[0] // slices
    return pl.pallas_call(
        encode_kernel,
        out_shape=jax.ShapeDtypeStruct((slices, rows + META, PW), jnp.int16),
        grid=(slices,),
        in_specs=[pl.BlockSpec((rows, PW), lambda i: (i, 0))],
        out_specs=pl.BlockSpec((1, rows + META, PW), lambda i: (i, 0, 0)),
        compiler_params=compiler_params(("arbitrary",)),
        cost_estimate=SHORT,
        name="encode_panel",
    )(base)


def slice_kernel(width, capacity, key_ref, code_ref, arrived_ref, out_ref, work, head, following):
    build_lists(key_ref, head, following, width)
    rows = work.shape[0]
    out_ref[pl.ds(rows, META), :] = jnp.zeros((META, out_ref.shape[1]), jnp.int16)
    for s in range(rows // TILE):
        spot = pl.ds(s * TILE, TILE)
        work[spot, :] = code_ref[spot, :].astype(I32).astype(F32) * row_scale(
            code_ref[pl.ds(rows, META), spot]
        )
        add_strip(key_ref, arrived_ref, work, head, following, s, width, capacity, s * TILE)
        write_code(out_ref, (), work[spot, :], rows, s)


def extend_slice(code, arrived, key, capacity):
    rows = code.shape[0] - META
    return pl.pallas_call(
        functools.partial(slice_kernel, PW // TILE, capacity),
        out_shape=jax.ShapeDtypeStruct(code.shape, jnp.int16),
        in_specs=[
            pl.BlockSpec(memory_space=pltpu.SMEM),
            pl.BlockSpec(memory_space=pltpu.VMEM),
            pl.BlockSpec(memory_space=pltpu.VMEM),
        ],
        out_specs=pl.BlockSpec(memory_space=pltpu.VMEM),
        scratch_shapes=[
            pltpu.VMEM((rows, PW), F32),
            pltpu.SMEM((rows // TILE,), I32),
            pltpu.SMEM((key.shape[0],), I32),
        ],
        compiler_params=compiler_params(),
        cost_estimate=SHORT,
        name="extend_slice",
    )(key, code, arrived)


def panel_kernel(width, capacity, key_ref, base_ref, arrived_ref, out_ref, work, head, following):
    step = pl.program_id(0)

    @pl.when(step == 0)
    def _():
        build_lists(key_ref, head, following, width)

    work[...] = base_ref[...]
    rows = base_ref.shape[0]
    strips = rows // TILE
    out_ref[0, pl.ds(rows, META), :] = jnp.zeros((META, out_ref.shape[2]), jnp.int16)
    for s in range(strips):
        add_strip(
            key_ref, arrived_ref, work, head, following, step * strips + s, width, capacity, s * TILE
        )
        write_code(out_ref, (0,), work[pl.ds(s * TILE, TILE), :], rows, s)


def code_panel(base, arrived, key, capacity, slices):
    rows = base.shape[0] // slices
    width = PW // TILE
    return pl.pallas_call(
        functools.partial(panel_kernel, width, capacity),
        out_shape=jax.ShapeDtypeStruct((slices, rows + META, PW), jnp.int16),
        grid_spec=pltpu.PrefetchScalarGridSpec(
            num_scalar_prefetch=1,
            grid=(slices,),
            in_specs=[
                pl.BlockSpec((rows, PW), lambda i, k: (i, 0)),
                pl.BlockSpec(memory_space=pltpu.VMEM),
            ],
            out_specs=pl.BlockSpec((1, rows + META, PW), lambda i, k: (i, 0, 0)),
            scratch_shapes=[
                pltpu.VMEM((rows, PW), F32),
                pltpu.SMEM((base.shape[0] // TILE,), I32),
                pltpu.SMEM((key.shape[0],), I32),
            ],
        ),
        compiler_params=compiler_params(("arbitrary",)),
        name="code_panel",
    )(key, base, arrived)


def split(x):
    high = x.astype(BF16)
    return high, (x - high.astype(F32)).astype(BF16)


def right_kernel(flag_ref, id_ref, pivot_ref, *refs):
    pieces, (high_ref, low_ref, upper_ref) = refs[:-3], refs[-3:]
    step = pl.program_id(0)
    height, columns = pieces[0].shape
    for p, piece in enumerate(pieces):
        upper_ref[pl.ds(pl.multiple_of(id_ref[p] * height, 8), height), :] = piece[...]
    row = lax.broadcasted_iota(I32, (PW, columns), 0)
    column = lax.broadcasted_iota(I32, (PW, columns), 1) + step * columns
    in_panel = jnp.logical_and(column < PW, flag_ref[1] == 0)
    upper = jnp.where(in_panel, jnp.where(row == column, -1.0, 0.0), upper_ref[...])
    a, b = split(pivot_ref[...])
    c, d = split(upper)
    right = (
        jnp.dot(a, d, preferred_element_type=F32) + jnp.dot(b, c, preferred_element_type=F32)
    ) + jnp.dot(a, c, preferred_element_type=F32)
    high_ref[...], low_ref[...] = split(right)


def right_factor(flags, ids, pivot_inverse, pieces):
    height, columns = pieces[0].shape
    block = min(512, columns)
    spec = pl.BlockSpec((PW, block), lambda i, f, s: (0, i))
    return pl.pallas_call(
        right_kernel,
        out_shape=[jax.ShapeDtypeStruct((PW, columns), t) for t in (BF16, BF16, F32)],
        grid_spec=pltpu.PrefetchScalarGridSpec(
            num_scalar_prefetch=2,
            grid=(columns // block,),
            in_specs=[pl.BlockSpec((PW, PW), lambda i, f, s: (0, 0))]
            + [pl.BlockSpec((height, block), lambda i, f, s: (0, i))] * len(pieces),
            out_specs=[spec, spec, spec],
        ),
        compiler_params=compiler_params(("arbitrary",)),
        cost_estimate=SHORT,
        name="right_factor",
    )(flags, ids, pivot_inverse, *pieces)


def update_kernel(block, per_slice, flag_ref, slice_ref, base_ref, code_ref, scale_ref, high_ref, low_ref, upper_ref, *refs):
    out_ref, token_ref = refs[-2:]
    step = pl.program_id(0)

    @pl.when(step == 0)
    def _():
        token_ref[...] = jnp.zeros_like(token_ref)

    row_block = slice_ref[step // per_slice] * per_slice + lax.rem(step, per_slice)
    above = jnp.logical_and(flag_ref[0] == 0, row_block < PW // block)

    @pl.when(above)
    def _():
        out_ref[:, pl.ds(PW, out_ref.shape[1] - PW)] = upper_ref[:, pl.ds(PW, out_ref.shape[1] - PW)]
        out_ref[:, pl.ds(0, PW)] = jnp.where(flag_ref[1] == 0, base_ref[:, pl.ds(0, PW)], upper_ref[:, pl.ds(0, PW)])

    @pl.when(jnp.logical_not(above))
    def _():
        code = code_ref[0].astype(I32)
        upper_part = (code + 128) >> 8
        lower_part = (code - upper_part * 256).astype(F32).astype(BF16)
        upper_part = (upper_part * 256).astype(F32).astype(BF16)
        high, low = high_ref[...], low_ref[...]
        product = (
            jnp.dot(lower_part, high, preferred_element_type=F32)
            + jnp.dot(upper_part, low, preferred_element_type=F32)
        ) + jnp.dot(upper_part, high, preferred_element_type=F32)
        for s in range(block // TILE):
            scale = row_scale(scale_ref[0, :, pl.ds(s * TILE, TILE)])
            rows = slice(s * TILE, (s + 1) * TILE)
            update = scale * product[rows]
            out_ref[pl.ds(s * TILE, TILE), pl.ds(PW, out_ref.shape[1] - PW)] = (
                base_ref[pl.ds(s * TILE, TILE), pl.ds(PW, out_ref.shape[1] - PW)] - update[:, PW:]
            )
            kept = jnp.where(flag_ref[1] == 0, 0.0, 1.0)
            out_ref[pl.ds(s * TILE, TILE), pl.ds(0, PW)] = (
                base_ref[pl.ds(s * TILE, TILE), pl.ds(0, PW)] * kept - update[:, :PW]
            )


def update_rows(flags, slice_ids, base, codes, high, low, upper, into=None):
    rows, columns = base.shape
    slices, slice_rows, _ = codes.shape
    slice_rows -= META
    block = min(256, slice_rows)
    per_slice = slice_rows // block

    if into is None:
        extra, aliases = [], {}
    elif into is base:
        extra, aliases = [], {2: 0}
    else:
        extra, aliases = [into], {8: 0}

    def base_map(i, f, s):
        return (s[i // per_slice] * per_slice + lax.rem(i, per_slice), 0)

    return pl.pallas_call(
        functools.partial(update_kernel, block, per_slice),
        out_shape=[jax.ShapeDtypeStruct((rows, columns), F32), jax.ShapeDtypeStruct((8, TILE), F32)],
        grid_spec=pltpu.PrefetchScalarGridSpec(
            num_scalar_prefetch=2,
            grid=(slices * per_slice,),
            in_specs=[
                pl.BlockSpec((block, columns), base_map),
                pl.BlockSpec((1, block, PW), lambda i, f, s: (i // per_slice, lax.rem(i, per_slice), 0)),
                pl.BlockSpec(
                    (1, META, block),
                    lambda i, f, s: (i // per_slice, slice_rows // META, lax.rem(i, per_slice)),
                ),
                pl.BlockSpec((PW, columns), lambda i, f, s: (0, 0)),
                pl.BlockSpec((PW, columns), lambda i, f, s: (0, 0)),
                pl.BlockSpec(
                    (block, columns), lambda i, f, s: (jnp.minimum(base_map(i, f, s)[0], PW // block - 1), 0)
                ),
            ]
            + [pl.BlockSpec(memory_space=pl.ANY)] * len(extra),
            out_specs=[
                pl.BlockSpec((block, columns), base_map),
                pl.BlockSpec((8, TILE), lambda i, f, s: (0, 0)),
            ],
        ),
        input_output_aliases=aliases,
        cost_estimate=pl.CostEstimate(
            flops=6 * slices * slice_rows * PW * columns,
            bytes_accessed=8 * slices * slice_rows * columns,
            transcendentals=0,
        ),
        compiler_params=compiler_params(("arbitrary",)),
        name="update_rows",
    )(flags, slice_ids, base, codes, codes, high, low, upper, *extra)


def gate(x, *earlier):
    anywhere = pl.BlockSpec(memory_space=pl.ANY)
    return pl.pallas_call(
        lambda *refs: None,
        out_shape=jax.ShapeDtypeStruct(x.shape, x.dtype),
        in_specs=[anywhere] * (1 + len(earlier)),
        out_specs=anywhere,
        input_output_aliases={0: 0},
        cost_estimate=pl.CostEstimate(flops=0, bytes_accessed=0, transcendentals=0),
        name="gate",
    )(x, *earlier)


def ring_order(count):
    return list(range(0, count, 2)) + list(range(count - 1, 0, -2))


def ring_gather(own, axis, before=()):
    count = lax.axis_size(axis)
    order = ring_order(count)
    ahead = [(order[i], order[(i + 1) % count]) for i in range(count)]
    back = [(b, a) for a, b in ahead]
    place = {d: p for p, d in enumerate(order)}
    steps = [0] + [s for t in range(1, count // 2) for s in (-t, t)] + [count // 2]
    whose = jnp.array([[order[(place[d] + s) % count] for s in steps] for d in range(count)], I32)
    whose = lax.dynamic_index_in_dim(whose, lax.axis_index(axis), keepdims=False)
    pieces = [own]
    left = right = own
    for step in range(1, count // 2):
        if step in before:
            left = gate(left, before[step])
        left, right = lax.ppermute(left, axis, ahead), lax.ppermute(right, axis, back)
        pieces += [left, right]
    half = own.shape[0] // 2
    if count // 2 in before:
        left = gate(left, before[count // 2])
    pieces.append(
        jnp.concatenate([lax.ppermute(left[:half], axis, ahead), lax.ppermute(right[half:], axis, back)], 0)
    )
    return pieces, whose


def scatter_first(parts, axis):
    count = lax.axis_size(axis)
    index = lax.axis_index(axis)
    odd = lax.ppermute(jnp.concatenate([parts[k : k + 1] for k in range(1, count, 2)]), axis, [(0, 1)])
    sent = [lax.ppermute(parts[k], axis, [(0, k)]) for k in range(2, count, 2)]
    sent += [lax.ppermute(odd[k // 2], axis, [(1, k)]) for k in range(3, count, 2)]
    mine = jnp.where(index == 0, parts[0], odd[0])
    for x in sent:
        mine = mine + x
    return mine


def tree_broadcast(block, axis):
    count = lax.axis_size(axis)
    index = lax.axis_index(axis)
    reach = count // 2
    while reach >= 1:
        sent = lax.ppermute(block, axis, [(i, i + reach) for i in range(0, count, 2 * reach)])
        block = jnp.where(index % (2 * reach) == reach, sent, block)
        reach //= 2
    return block


def spread_pivots(parent, axis):
    count = lax.axis_size(axis)
    height = PW // count
    mine = parent[:height]
    index = lax.axis_index(axis)
    received = mine
    for k in range(1, count):
        sent = lax.ppermute(parent[k * height : (k + 1) * height], axis, [(0, k)])
        received = jnp.where(index == k, sent, received)
    return received


def gather_pieces(piece, axis):
    count = lax.axis_size(axis)
    pieces, ids = [piece], [lax.axis_index(axis)]
    reach = count // 2
    while reach >= 1:
        pairs = [(i, i ^ reach) for i in range(count)]
        pieces = pieces + [lax.ppermute(x, axis, pairs) for x in pieces]
        ids = ids + [i ^ reach for i in ids]
        reach //= 2
    return pieces, jnp.stack(ids)


def plain_path(flags, parent, child, owner, slot, pivot_inverse):
    bulk_count, column_count = lax.axis_size("bulk"), lax.axis_size("col")
    devices = bulk_count * column_count
    rows, columns = parent.shape
    capacity = max(2, 2 * child.shape[0] // devices)
    width = columns // TILE
    outgoing = pack(owner, slot, child, devices, capacity)
    arrived = lax.all_to_all(outgoing, ("bulk", "col"), split_axis=0, concat_axis=0, tiled=True)
    slots = read_slots(arrived, capacity)
    strip, tile_column = slots // width, slots % width
    pivot_tiles = PW // TILE
    panel_key = jnp.where((slots >= 0) & (tile_column < pivot_tiles), strip * pivot_tiles + tile_column, -1)
    pivot_key = jnp.where((slots >= 0) & (strip < pivot_tiles), slots, -1)

    codes = code_panel(parent, arrived, panel_key, capacity, column_count)
    upper = tree_broadcast(extend(parent, arrived, pivot_key, width, capacity, PW, columns), "bulk")
    high, low, upper = right_factor(flags, jnp.zeros((1,), I32), pivot_inverse, [upper])
    pieces, whose = ring_gather(scatter_first(codes, "col"), "col")
    extended = extend(parent, arrived, slots, width, capacity, rows, columns)
    return update_rows(flags, whose, extended, jnp.stack(pieces), high, low, upper, into=extended)[0]


def quick_path(plan, flags, parent, child, owner, slot, pivot_inverse):
    bulk_count, column_count = lax.axis_size("bulk"), lax.axis_size("col")
    width, half, groups, share = plan["width"], plan["half"], plan["groups"], plan["early"]
    swap = [(i, i ^ half) for i in range(column_count)]
    halves = [
        [b * column_count + h * half + c for b in range(bulk_count) for c in range(half)] for h in range(2)
    ]

    def exchange(blocks, groups=None):
        return lax.all_to_all(
            blocks, ("bulk", "col"), split_axis=0, concat_axis=0, axis_index_groups=groups, tiled=True
        )

    early, near, far, over = sort_children(plan, owner, slot, flags, child)
    far = lax.ppermute(far, "col", swap)
    early = exchange(early)
    code = scatter_first(encode_panel(parent, column_count), "col")
    pivots = spread_pivots(parent, "bulk")

    codes = read_slots(early, share)
    panel_key = jnp.where((codes >= plan["panel_code"]) & (codes < plan["pivot_code"]), codes - plan["panel_code"], -1)
    pivot_key = jnp.where(codes >= plan["pivot_code"], codes - plan["pivot_code"], -1)
    plain_key = jnp.where(codes < plan["panel_code"], codes, -1)
    code = extend_slice(gate(code, pivots, far), early, panel_key, share)
    pivots = extend(pivots, early, pivot_key, width, share, *pivots.shape)
    uppers, ids = gather_pieces(pivots, "bulk")
    high, low, upper = right_factor(flags, ids, pivot_inverse, uppers)
    pieces, whose = ring_gather(code, "col", {column_count // 2 - 1: high})
    cut = len(pieces) - 3
    result, done = update_rows(flags, whose[:cut], parent, jnp.stack(pieces[:cut]), high, low, upper)

    late = distribute([near, far], over, groups, plan["late"])
    late = exchange(gate(late, *pieces[-3:]), halves)
    result, _ = update_rows(flags, whose[cut:], parent, jnp.stack(pieces[cut:]), high, low, upper, into=result)
    result = touch_tiles(result, early, plain_key, width, share)

    over = jnp.full((8, TILE), read_over(late, plan["late"]), I32)
    over = jnp.max(jnp.maximum(over, lax.ppermute(over, "col", swap)))
    return touch_tiles(result, late, read_slots(late, plan["late"]), width, plan["late"]), over


def make_plan(bulk_count, column_count, rows, columns, child_count):
    strips, width, pivot = rows // TILE, columns // TILE, PW // TILE
    if pivot % bulk_count or strips % column_count or column_count % 4:
        return None
    half = column_count // 2
    share = child_count // 2
    panel_strips, pivot_strips = strips // column_count, pivot // bulk_count
    panel_code = strips * width
    return dict(
        devices=bulk_count * column_count,
        columns=column_count,
        width=width,
        pivot=pivot,
        half=half,
        groups=bulk_count * half,
        early=max(2, child_count // (bulk_count * column_count)),
        listed=max(8, share * 7 // 16),
        late=12,
        panel_strips=panel_strips,
        pivot_strips=pivot_strips,
        panel_code=panel_code,
        pivot_code=panel_code + panel_strips * pivot,
    )


def per_device(parent, child, owner, slot, pivot_inverse):
    flags = jnp.stack([lax.axis_index("bulk"), lax.axis_index("col")]).astype(I32)
    owner = owner[:, 0]
    plan = make_plan(
        lax.axis_size("bulk"), lax.axis_size("col"), parent.shape[0], parent.shape[1], child.shape[0]
    )
    if plan is None:
        return plain_path(flags, parent, child, owner, slot, pivot_inverse)
    result, over = quick_path(plan, flags, parent, child, owner, slot, pivot_inverse)

    def again(state):
        return jnp.int32(0), plain_path(flags, parent, child, owner, slot, pivot_inverse)

    return lax.while_loop(lambda state: state[0] > 0, again, (over, result))[1]


def solution(mesh):
    in_specs = (
        P("bulk", "col"),
        P(("bulk", "col"), None, None),
        P(("bulk", "col"), None),
        P(("bulk", "col")),
        P(),
    )
    return jax.shard_map(
        per_device, mesh=mesh, in_specs=in_specs, out_specs=P("bulk", "col"), check_vma=False
    )
```

```python
import functools

import jax
import jax.numpy as jnp
from jax import lax
from jax.experimental import pallas as pl
from jax.experimental.pallas import tpu as pltpu
from jax.sharding import PartitionSpec as P

PW = 512
TILE = 128
META = 16
CODE_TOP = 32600.0
VMEM_LIMIT = 56 * 1024 * 1024

SHORT = pl.CostEstimate(flops=0, bytes_accessed=4096, transcendentals=0)

F32 = jnp.float32
BF16 = jnp.bfloat16
I32 = jnp.int32


def compiler_params(semantics=None):
    return pltpu.CompilerParams(dimension_semantics=semantics, vmem_limit_bytes=VMEM_LIMIT)


def pack_kernel(devices, capacity, owner_ref, slot_ref, child_ref, out_ref, filled, slots, meta, sem, meta_sem):
    child_count = owner_ref.shape[0]

    def clear(d, _):
        filled[d] = 0
        return 0

    lax.fori_loop(0, devices, clear, 0)

    def clear_slot(i, _):
        slots[i] = -1
        return 0

    lax.fori_loop(0, devices * capacity, clear_slot, 0)

    def place(i, _):
        d = owner_ref[i]
        k = filled[d]
        filled[d] = k + 1
        slots[d * capacity + k] = slot_ref[i]
        pltpu.make_async_copy(
            child_ref.at[i], out_ref.at[d, pl.ds(pl.multiple_of(k * TILE, TILE), TILE)], sem
        ).start()
        return 0

    lax.fori_loop(0, child_count, place, 0)
    lane = lax.broadcasted_iota(I32, (META, TILE), 1)
    row = lax.broadcasted_iota(I32, (META, TILE), 0)

    def write_meta(d, _):
        value = jnp.full((META, TILE), -1, I32)
        for k in range(capacity):
            value = jnp.where(lane == k, slots[d * capacity + k], value)
        coded = jnp.where(row == 0, value >> 4, value & 15)
        meta[d] = coded.astype(F32).astype(BF16)
        return 0

    lax.fori_loop(0, devices, write_meta, 0)
    copy = pltpu.make_async_copy(meta, out_ref.at[:, pl.ds(capacity * TILE, META)], meta_sem)
    copy.start()
    pltpu.make_async_copy(child_ref, child_ref, sem).wait()
    copy.wait()


def pack(owner, slot, child, devices, capacity):
    rows = capacity * TILE + META
    return pl.pallas_call(
        functools.partial(pack_kernel, devices, capacity),
        out_shape=jax.ShapeDtypeStruct((devices, rows, TILE), BF16),
        in_specs=[
            pl.BlockSpec(memory_space=pltpu.SMEM),
            pl.BlockSpec(memory_space=pltpu.SMEM),
            pl.BlockSpec(memory_space=pltpu.VMEM),
        ],
        out_specs=pl.BlockSpec(memory_space=pl.ANY),
        scratch_shapes=[
            pltpu.SMEM((devices,), I32),
            pltpu.SMEM((devices * capacity,), I32),
            pltpu.VMEM((devices, META, TILE), BF16),
            pltpu.SemaphoreType.DMA,
            pltpu.SemaphoreType.DMA,
        ],
        compiler_params=compiler_params(),
        name="pack_children",
    )(owner, slot, child)


def lanes(values, count, fallback=-1):
    lane = lax.broadcasted_iota(I32, (META, TILE), 1)
    out = jnp.full((META, TILE), fallback, I32)
    for k in range(count):
        out = jnp.where(lane == k, values(k), out)
    return out


def coded_lines(code, third):
    row = lax.broadcasted_iota(I32, (META, TILE), 0)
    lines = jnp.where(row == 0, code >> 4, jnp.where(row == 1, code & 15, third))
    return lines.astype(F32).astype(BF16)


def fill(ref, count, value):
    def step(i, _):
        ref[i] = value
        return 0

    lax.fori_loop(0, count, step, 0, unroll=8 if count % 8 == 0 else 1)


def sort_kernel(
    plan, kind_ref, dest_ref, code_ref, child_ref,
    early_ref, near_ref, far_ref, over_ref,
    filled, early_code, list_code, list_dest, early_meta, list_meta, sem, meta_sem,
):
    devices, share, size, half = plan["devices"], plan["early"], plan["listed"], plan["half"]
    columns = plan["columns"]
    lists = (near_ref, far_ref)
    fill(filled, devices + 2, 0)
    fill(early_code, devices * share, -1)
    fill(list_code, 2 * size, -1)
    fill(list_dest, 2 * size, -1)
    over_ref[0] = 0

    def send_early(i, dest, k):
        early_code[dest * share + k] = code_ref[i]
        rows = pl.ds(pl.multiple_of(k * TILE, TILE), TILE)
        pltpu.make_async_copy(child_ref.at[i], early_ref.at[dest, rows], sem).start()

    def place_special(i, _):
        @pl.when(kind_ref[i] == 2)
        def _():
            dest = dest_ref[i]
            k = filled[dest]
            filled[dest] = k + 1

            @pl.when(k >= share)
            def _():
                over_ref[0] = 1

            send_early(i, dest, jnp.minimum(k, share - 1))

        return 0

    def place_plain(i, _):
        kind, dest = kind_ref[i], dest_ref[i]

        @pl.when(kind < 2)
        def _():
            k = filled[dest]
            filled[dest] = k + 1

            @pl.when(k < share)
            def _():
                send_early(i, dest, k)

            @pl.when(k >= share)
            def _():
                spot = filled[devices + kind]
                filled[devices + kind] = spot + 1

                @pl.when(spot >= size)
                def _():
                    over_ref[0] = 1

                spot = jnp.minimum(spot, size - 1)
                list_code[kind * size + spot] = code_ref[i]
                list_dest[kind * size + spot] = (dest // columns) * half + lax.rem(dest, half)
                rows = pl.ds(pl.multiple_of(spot * TILE, TILE), TILE)
                for which in range(2):

                    @pl.when(kind == which)
                    def _(which=which):
                        pltpu.make_async_copy(child_ref.at[i], lists[which].at[rows], sem).start()

        return 0

    lax.fori_loop(0, kind_ref.shape[0], place_special, 0)
    lax.fori_loop(0, kind_ref.shape[0], place_plain, 0)
    copies = []
    for which in range(2):
        code = lanes(lambda k: list_code[which * size + k], size)
        dest = lanes(lambda k: list_dest[which * size + k], size)
        list_meta[which] = coded_lines(code, dest)
        copies.append(
            pltpu.make_async_copy(
                list_meta.at[which], lists[which].at[pl.ds(size * TILE, META)], meta_sem.at[which]
            )
        )
        copies[-1].start()

    def write_meta(d, _):
        early_meta[d] = coded_lines(lanes(lambda k: early_code[d * share + k], share), 0)
        return 0

    lax.fori_loop(0, devices, write_meta, 0)
    copies.append(
        pltpu.make_async_copy(early_meta, early_ref.at[:, pl.ds(share * TILE, META)], meta_sem.at[2])
    )
    copies[-1].start()
    pltpu.make_async_copy(child_ref, child_ref, sem).wait()
    for copy in copies:
        copy.wait()


def sort_children(plan, owner, slot, flags, child):
    devices, share, listed = plan["devices"], plan["early"], plan["listed"]
    bulk, col = owner // plan["columns"], owner % plan["columns"]
    strip, tile = slot // plan["width"], slot % plan["width"]
    pivot = (bulk == 0) & (strip < plan["pivot"])
    panel = (col == 0) & (tile < plan["pivot"])
    pivot, panel = pivot & ~panel, panel & ~pivot
    bulk = jnp.where(pivot, strip // plan["pivot_strips"], bulk)
    col = jnp.where(panel, strip // plan["panel_strips"], col)
    code = jnp.where(panel, plan["panel_code"] + (strip % plan["panel_strips"]) * plan["pivot"] + tile, slot)
    code = jnp.where(pivot, plan["pivot_code"] + (strip % plan["pivot_strips"]) * plan["width"] + tile, code)
    here = col // plan["half"] == flags[1] // plan["half"]
    kind = jnp.where(pivot | panel, 2, jnp.where(here, 0, 1))
    dest = bulk * plan["columns"] + col
    anywhere = pl.BlockSpec(memory_space=pl.ANY)
    scalars = pl.BlockSpec(memory_space=pltpu.SMEM)
    in_list = jax.ShapeDtypeStruct((listed * TILE + META, TILE), BF16)
    return pl.pallas_call(
        functools.partial(sort_kernel, plan),
        out_shape=[
            jax.ShapeDtypeStruct((devices, share * TILE + META, TILE), BF16),
            in_list,
            in_list,
            jax.ShapeDtypeStruct((1,), I32),
        ],
        in_specs=[scalars, scalars, scalars, pl.BlockSpec(memory_space=pltpu.VMEM)],
        out_specs=[anywhere, anywhere, anywhere, scalars],
        scratch_shapes=[
            pltpu.SMEM((devices + 2,), I32),
            pltpu.SMEM((devices * share,), I32),
            pltpu.SMEM((2 * listed,), I32),
            pltpu.SMEM((2 * listed,), I32),
            pltpu.VMEM((devices, META, TILE), BF16),
            pltpu.VMEM((2, META, TILE), BF16),
            pltpu.SemaphoreType.DMA,
            pltpu.SemaphoreType.DMA((3,)),
        ],
        compiler_params=compiler_params(),
        cost_estimate=SHORT,
        name="sort_children",
    )(kind, dest, code, child)


def read_list(listed):
    count = (listed.shape[0] - META) // TILE
    lines = listed[count * TILE : count * TILE + 3, :count].astype(I32)
    return lines[0] * 16 + lines[1], lines[2]


def distribute_kernel(groups, capacity, sizes, *refs):
    n = len(sizes)
    code_refs, dest_refs, block_refs = refs[:n], refs[n : 2 * n], refs[2 * n : 3 * n]
    over_in, out_ref, over_ref, filled, codes, meta, spare, sem, meta_sem = refs[3 * n :]
    fill(filled, groups, 0)
    fill(codes, groups * capacity, -1)
    over_ref[0] = over_in[0]
    for code_ref, dest_ref, block_ref, size in zip(code_refs, dest_refs, block_refs, sizes):

        def place(i, _, code_ref=code_ref, dest_ref=dest_ref, block_ref=block_ref):
            dest = dest_ref[i]
            block = block_ref.at[pl.ds(pl.multiple_of(i * TILE, TILE), TILE)]

            @pl.when(dest >= 0)
            def _():
                k = filled[dest]
                filled[dest] = k + 1

                @pl.when(k >= capacity)
                def _():
                    over_ref[0] = 1

                k = jnp.minimum(k, capacity - 1)
                codes[dest * capacity + k] = code_ref[i]
                pltpu.make_async_copy(
                    block, out_ref.at[dest, pl.ds(pl.multiple_of(k * TILE, TILE), TILE)], sem
                ).start()

            @pl.when(dest < 0)
            def _():
                pltpu.make_async_copy(block, spare, sem).start()

            return 0

        lax.fori_loop(0, size, place, 0)

    def write_meta(g, _):
        meta[g] = coded_lines(lanes(lambda k: codes[g * capacity + k], capacity), over_ref[0])
        return 0

    lax.fori_loop(0, groups, write_meta, 0)
    copy = pltpu.make_async_copy(meta, out_ref.at[:, pl.ds(capacity * TILE, META)], meta_sem)
    copy.start()
    for block_ref, size in zip(block_refs, sizes):
        blocks = block_ref.at[pl.ds(0, size * TILE)]
        pltpu.make_async_copy(blocks, blocks, sem).wait()
    copy.wait()


def distribute(lists, over, groups, capacity):
    sizes = [(x.shape[0] - META) // TILE for x in lists]
    codes, dests = zip(*[read_list(x) for x in lists])
    n = len(lists)
    return pl.pallas_call(
        functools.partial(distribute_kernel, groups, capacity, sizes),
        out_shape=[
            jax.ShapeDtypeStruct((groups, capacity * TILE + META, TILE), BF16),
            jax.ShapeDtypeStruct((1,), I32),
        ],
        in_specs=[pl.BlockSpec(memory_space=pltpu.SMEM)] * (2 * n)
        + [pl.BlockSpec(memory_space=pltpu.VMEM)] * n
        + [pl.BlockSpec(memory_space=pltpu.SMEM)],
        out_specs=[pl.BlockSpec(memory_space=pl.ANY), pl.BlockSpec(memory_space=pltpu.SMEM)],
        scratch_shapes=[
            pltpu.SMEM((groups,), I32),
            pltpu.SMEM((groups * capacity,), I32),
            pltpu.VMEM((groups, META, TILE), BF16),
            pltpu.VMEM((TILE, TILE), BF16),
            pltpu.SemaphoreType.DMA,
            pltpu.SemaphoreType.DMA,
        ],
        compiler_params=compiler_params(),
        cost_estimate=SHORT,
        name="distribute",
    )(*codes, *dests, *lists, over)[0]


def read_over(arrived, capacity):
    return jnp.max(arrived[:, capacity * TILE + 2, 0].astype(I32))


def read_slots(arrived, capacity):
    coded = arrived[:, capacity * TILE : capacity * TILE + 2, :capacity].astype(I32)
    return (coded[:, 0] * 16 + coded[:, 1]).reshape(-1)


def build_lists(key_ref, head, following, width):
    def clear(i, _):
        head[i] = -1
        return 0

    lax.fori_loop(0, head.shape[0], clear, 0)

    def add(i, _):
        key = key_ref[i]

        @pl.when(key >= 0)
        def _():
            strip = key // width
            following[i] = head[strip]
            head[strip] = i

        return 0

    lax.fori_loop(0, key_ref.shape[0], add, 0)


def add_strip(key_ref, arrived_ref, out, head, following, strip, width, capacity, row):
    def body(i):
        column = pl.multiple_of((key_ref[i] % width) * TILE, TILE)
        start = pl.multiple_of((i % capacity) * TILE, TILE)
        block = arrived_ref[i // capacity, pl.ds(start, TILE), :]
        spot = (pl.ds(row, TILE), pl.ds(column, TILE))
        out[spot] = out[spot] + block.astype(F32)
        return following[i]

    lax.while_loop(lambda i: i >= 0, body, head[strip])


def extend_kernel(width, capacity, key_ref, base_ref, arrived_ref, out_ref, head, following):
    step = pl.program_id(0)

    @pl.when(step == 0)
    def _():
        build_lists(key_ref, head, following, width)

    out_ref[...] = base_ref[...]
    strips = base_ref.shape[0] // TILE
    for s in range(strips):
        add_strip(
            key_ref, arrived_ref, out_ref, head, following, step * strips + s, width, capacity, s * TILE
        )


def extend(base, arrived, key, width, capacity, rows, columns):
    return pl.pallas_call(
        functools.partial(extend_kernel, width, capacity),
        out_shape=jax.ShapeDtypeStruct((rows, columns), F32),
        grid_spec=pltpu.PrefetchScalarGridSpec(
            num_scalar_prefetch=1,
            grid=(rows // TILE,),
            in_specs=[
                pl.BlockSpec((TILE, columns), lambda i, k: (i, 0)),
                pl.BlockSpec(memory_space=pltpu.VMEM),
            ],
            out_specs=pl.BlockSpec((TILE, columns), lambda i, k: (i, 0)),
            scratch_shapes=[
                pltpu.SMEM((rows // TILE,), I32),
                pltpu.SMEM((key.shape[0],), I32),
            ],
        ),
        compiler_params=compiler_params(("arbitrary",)),
        cost_estimate=pl.CostEstimate(flops=rows * columns, bytes_accessed=12 * rows * columns, transcendentals=0),
        name="extend_add",
    )(key, base, arrived)


AHEAD = 24
BUFFERS = 48


def touch_kernel(
    width, capacity, key_ref, base_ref, arrived_ref, out_ref,
    tiles, head, following, active, read_sem, write_sem,
):
    del base_ref
    fill(head, head.shape[0], -1)

    def chain(i, count):
        key = key_ref[i]
        at = jnp.maximum(key, 0)
        first = jnp.logical_and(key >= 0, head[at] < 0)

        @pl.when(key >= 0)
        def _():
            following[i] = head[at]
            head[at] = i

        @pl.when(first)
        def _():
            active[count] = key

        return count + first.astype(I32)

    count = lax.fori_loop(0, key_ref.shape[0], chain, jnp.int32(0))

    def copy(j, out):
        key = active[j]
        slot = lax.rem(j, BUFFERS)
        place = out_ref.at[
            pl.ds(pl.multiple_of((key // width) * TILE, TILE), TILE),
            pl.ds(pl.multiple_of((key % width) * TILE, TILE), TILE),
        ]
        if out:
            return pltpu.make_async_copy(tiles.at[slot], place, write_sem.at[slot])
        return pltpu.make_async_copy(place, tiles.at[slot], read_sem.at[slot])

    def first_reads(j, _):
        copy(j, False).start()
        return 0

    lax.fori_loop(0, jnp.minimum(count, AHEAD), first_reads, 0)

    def step(j, _):
        later = j + AHEAD

        @pl.when(later < count)
        def _():
            @pl.when(later >= BUFFERS)
            def _():
                copy(later - BUFFERS, True).wait()

            copy(later, False).start()

        copy(j, False).wait()
        slot = lax.rem(j, BUFFERS)

        def body(i):
            start = pl.multiple_of((i % capacity) * TILE, TILE)
            tiles[slot] = tiles[slot] + arrived_ref[i // capacity, pl.ds(start, TILE), :].astype(F32)
            return following[i]

        lax.while_loop(lambda i: i >= 0, body, head[active[j]])
        copy(j, True).start()
        return 0

    lax.fori_loop(0, count, step, 0)

    def last_writes(j, _):
        copy(j, True).wait()
        return 0

    lax.fori_loop(jnp.maximum(count - BUFFERS, 0), count, last_writes, 0)


def touch_tiles(base, arrived, key, width, capacity):
    rows, columns = base.shape
    return pl.pallas_call(
        functools.partial(touch_kernel, width, capacity),
        out_shape=jax.ShapeDtypeStruct((rows, columns), F32),
        in_specs=[
            pl.BlockSpec(memory_space=pltpu.SMEM),
            pl.BlockSpec(memory_space=pl.ANY),
            pl.BlockSpec(memory_space=pltpu.VMEM),
        ],
        out_specs=pl.BlockSpec(memory_space=pl.ANY),
        scratch_shapes=[
            pltpu.VMEM((BUFFERS, TILE, TILE), F32),
            pltpu.SMEM((rows * columns // (TILE * TILE),), I32),
            pltpu.SMEM((key.shape[0],), I32),
            pltpu.SMEM((key.shape[0],), I32),
            pltpu.SemaphoreType.DMA((BUFFERS,)),
            pltpu.SemaphoreType.DMA((BUFFERS,)),
        ],
        input_output_aliases={1: 0},
        compiler_params=compiler_params(),
        name="touch_tiles",
    )(key, base, arrived)


def code_rows(values):
    top = jnp.maximum(jnp.max(jnp.abs(values), axis=1, keepdims=True), 1e-30)
    exponent = jnp.ceil(jnp.log2(top) * 64.0)
    code = jnp.round(values * (CODE_TOP * jnp.exp2(exponent * (-1.0 / 64.0))))
    return code.astype(I32), exponent


def diagonal(n):
    return lax.broadcasted_iota(I32, (n, n), 0) == lax.broadcasted_iota(I32, (n, n), 1)


def write_code(out_ref, lead, values, rows, s):
    code, exponent = code_rows(values)
    out_ref[(*lead, pl.ds(s * TILE, TILE), slice(None))] = code.astype(jnp.int16)
    line = jnp.sum(jnp.where(diagonal(TILE), exponent, 0.0), axis=0, keepdims=True)
    out_ref[(*lead, pl.ds(rows, META), pl.ds(s * TILE, TILE))] = (
        jnp.broadcast_to(line, (META, TILE)).astype(I32).astype(jnp.int16)
    )


def row_scale(lines):
    line = lines.astype(I32).astype(F32)[:1]
    exponent = jnp.sum(jnp.where(diagonal(TILE), line, 0.0), axis=1, keepdims=True)
    return jnp.exp2(exponent * (1.0 / 64.0)) * (1.0 / CODE_TOP)


def encode_kernel(base_ref, out_ref):
    rows = base_ref.shape[0]
    out_ref[0, pl.ds(rows, META), :] = jnp.zeros((META, out_ref.shape[2]), jnp.int16)
    for s in range(rows // TILE):
        write_code(out_ref, (0,), base_ref[pl.ds(s * TILE, TILE), :], rows, s)


def encode_panel(base, slices):
    rows = base.shape[0] // slices
    return pl.pallas_call(
        encode_kernel,
        out_shape=jax.ShapeDtypeStruct((slices, rows + META, PW), jnp.int16),
        grid=(slices,),
        in_specs=[pl.BlockSpec((rows, PW), lambda i: (i, 0))],
        out_specs=pl.BlockSpec((1, rows + META, PW), lambda i: (i, 0, 0)),
        compiler_params=compiler_params(("arbitrary",)),
        cost_estimate=SHORT,
        name="encode_panel",
    )(base)


def slice_kernel(width, capacity, key_ref, code_ref, arrived_ref, out_ref, work, head, following):
    build_lists(key_ref, head, following, width)
    rows = work.shape[0]
    out_ref[pl.ds(rows, META), :] = jnp.zeros((META, out_ref.shape[1]), jnp.int16)
    for s in range(rows // TILE):
        spot = pl.ds(s * TILE, TILE)
        work[spot, :] = code_ref[spot, :].astype(I32).astype(F32) * row_scale(
            code_ref[pl.ds(rows, META), spot]
        )
        add_strip(key_ref, arrived_ref, work, head, following, s, width, capacity, s * TILE)
        write_code(out_ref, (), work[spot, :], rows, s)


def extend_slice(code, arrived, key, capacity):
    rows = code.shape[0] - META
    return pl.pallas_call(
        functools.partial(slice_kernel, PW // TILE, capacity),
        out_shape=jax.ShapeDtypeStruct(code.shape, jnp.int16),
        in_specs=[
            pl.BlockSpec(memory_space=pltpu.SMEM),
            pl.BlockSpec(memory_space=pltpu.VMEM),
            pl.BlockSpec(memory_space=pltpu.VMEM),
        ],
        out_specs=pl.BlockSpec(memory_space=pltpu.VMEM),
        scratch_shapes=[
            pltpu.VMEM((rows, PW), F32),
            pltpu.SMEM((rows // TILE,), I32),
            pltpu.SMEM((key.shape[0],), I32),
        ],
        compiler_params=compiler_params(),
        cost_estimate=SHORT,
        name="extend_slice",
    )(key, code, arrived)


def panel_kernel(width, capacity, key_ref, base_ref, arrived_ref, out_ref, work, head, following):
    step = pl.program_id(0)

    @pl.when(step == 0)
    def _():
        build_lists(key_ref, head, following, width)

    work[...] = base_ref[...]
    rows = base_ref.shape[0]
    strips = rows // TILE
    out_ref[0, pl.ds(rows, META), :] = jnp.zeros((META, out_ref.shape[2]), jnp.int16)
    for s in range(strips):
        add_strip(
            key_ref, arrived_ref, work, head, following, step * strips + s, width, capacity, s * TILE
        )
        write_code(out_ref, (0,), work[pl.ds(s * TILE, TILE), :], rows, s)


def code_panel(base, arrived, key, capacity, slices):
    rows = base.shape[0] // slices
    width = PW // TILE
    return pl.pallas_call(
        functools.partial(panel_kernel, width, capacity),
        out_shape=jax.ShapeDtypeStruct((slices, rows + META, PW), jnp.int16),
        grid_spec=pltpu.PrefetchScalarGridSpec(
            num_scalar_prefetch=1,
            grid=(slices,),
            in_specs=[
                pl.BlockSpec((rows, PW), lambda i, k: (i, 0)),
                pl.BlockSpec(memory_space=pltpu.VMEM),
            ],
            out_specs=pl.BlockSpec((1, rows + META, PW), lambda i, k: (i, 0, 0)),
            scratch_shapes=[
                pltpu.VMEM((rows, PW), F32),
                pltpu.SMEM((base.shape[0] // TILE,), I32),
                pltpu.SMEM((key.shape[0],), I32),
            ],
        ),
        compiler_params=compiler_params(("arbitrary",)),
        name="code_panel",
    )(key, base, arrived)


def split(x):
    high = x.astype(BF16)
    return high, (x - high.astype(F32)).astype(BF16)


def right_kernel(flag_ref, id_ref, pivot_ref, *refs):
    pieces, (high_ref, low_ref, upper_ref) = refs[:-3], refs[-3:]
    step = pl.program_id(0)
    height, columns = pieces[0].shape
    for p, piece in enumerate(pieces):
        upper_ref[pl.ds(pl.multiple_of(id_ref[p] * height, 8), height), :] = piece[...]
    row = lax.broadcasted_iota(I32, (PW, columns), 0)
    column = lax.broadcasted_iota(I32, (PW, columns), 1) + step * columns
    in_panel = jnp.logical_and(column < PW, flag_ref[1] == 0)
    upper = jnp.where(in_panel, jnp.where(row == column, -1.0, 0.0), upper_ref[...])
    a, b = split(pivot_ref[...])
    c, d = split(upper)
    right = (
        jnp.dot(a, d, preferred_element_type=F32) + jnp.dot(b, c, preferred_element_type=F32)
    ) + jnp.dot(a, c, preferred_element_type=F32)
    high_ref[...], low_ref[...] = split(right)


def right_factor(flags, ids, pivot_inverse, pieces):
    height, columns = pieces[0].shape
    block = min(512, columns)
    spec = pl.BlockSpec((PW, block), lambda i, f, s: (0, i))
    return pl.pallas_call(
        right_kernel,
        out_shape=[jax.ShapeDtypeStruct((PW, columns), t) for t in (BF16, BF16, F32)],
        grid_spec=pltpu.PrefetchScalarGridSpec(
            num_scalar_prefetch=2,
            grid=(columns // block,),
            in_specs=[pl.BlockSpec((PW, PW), lambda i, f, s: (0, 0))]
            + [pl.BlockSpec((height, block), lambda i, f, s: (0, i))] * len(pieces),
            out_specs=[spec, spec, spec],
        ),
        compiler_params=compiler_params(("arbitrary",)),
        cost_estimate=SHORT,
        name="right_factor",
    )(flags, ids, pivot_inverse, *pieces)


def update_kernel(block, per_slice, flag_ref, slice_ref, base_ref, code_ref, scale_ref, high_ref, low_ref, upper_ref, *refs):
    out_ref, token_ref = refs[-2:]
    step = pl.program_id(0)

    @pl.when(step == 0)
    def _():
        token_ref[...] = jnp.zeros_like(token_ref)

    row_block = slice_ref[step // per_slice] * per_slice + lax.rem(step, per_slice)
    above = jnp.logical_and(flag_ref[0] == 0, row_block < PW // block)

    @pl.when(above)
    def _():
        out_ref[:, pl.ds(PW, out_ref.shape[1] - PW)] = upper_ref[:, pl.ds(PW, out_ref.shape[1] - PW)]
        out_ref[:, pl.ds(0, PW)] = jnp.where(flag_ref[1] == 0, base_ref[:, pl.ds(0, PW)], upper_ref[:, pl.ds(0, PW)])

    @pl.when(jnp.logical_not(above))
    def _():
        code = code_ref[0].astype(I32)
        upper_part = (code + 128) >> 8
        lower_part = (code - upper_part * 256).astype(F32).astype(BF16)
        upper_part = (upper_part * 256).astype(F32).astype(BF16)
        high, low = high_ref[...], low_ref[...]
        product = (
            jnp.dot(lower_part, high, preferred_element_type=F32)
            + jnp.dot(upper_part, low, preferred_element_type=F32)
        ) + jnp.dot(upper_part, high, preferred_element_type=F32)
        for s in range(block // TILE):
            scale = row_scale(scale_ref[0, :, pl.ds(s * TILE, TILE)])
            rows = slice(s * TILE, (s + 1) * TILE)
            update = scale * product[rows]
            out_ref[pl.ds(s * TILE, TILE), pl.ds(PW, out_ref.shape[1] - PW)] = (
                base_ref[pl.ds(s * TILE, TILE), pl.ds(PW, out_ref.shape[1] - PW)] - update[:, PW:]
            )
            kept = jnp.where(flag_ref[1] == 0, 0.0, 1.0)
            out_ref[pl.ds(s * TILE, TILE), pl.ds(0, PW)] = (
                base_ref[pl.ds(s * TILE, TILE), pl.ds(0, PW)] * kept - update[:, :PW]
            )


def update_rows(flags, slice_ids, base, codes, high, low, upper, into=None):
    rows, columns = base.shape
    slices, slice_rows, _ = codes.shape
    slice_rows -= META
    block = min(256, slice_rows)
    per_slice = slice_rows // block

    if into is None:
        extra, aliases = [], {}
    elif into is base:
        extra, aliases = [], {2: 0}
    else:
        extra, aliases = [into], {8: 0}

    def base_map(i, f, s):
        return (s[i // per_slice] * per_slice + lax.rem(i, per_slice), 0)

    return pl.pallas_call(
        functools.partial(update_kernel, block, per_slice),
        out_shape=[jax.ShapeDtypeStruct((rows, columns), F32), jax.ShapeDtypeStruct((8, TILE), F32)],
        grid_spec=pltpu.PrefetchScalarGridSpec(
            num_scalar_prefetch=2,
            grid=(slices * per_slice,),
            in_specs=[
                pl.BlockSpec((block, columns), base_map),
                pl.BlockSpec((1, block, PW), lambda i, f, s: (i // per_slice, lax.rem(i, per_slice), 0)),
                pl.BlockSpec(
                    (1, META, block),
                    lambda i, f, s: (i // per_slice, slice_rows // META, lax.rem(i, per_slice)),
                ),
                pl.BlockSpec((PW, columns), lambda i, f, s: (0, 0)),
                pl.BlockSpec((PW, columns), lambda i, f, s: (0, 0)),
                pl.BlockSpec(
                    (block, columns), lambda i, f, s: (jnp.minimum(base_map(i, f, s)[0], PW // block - 1), 0)
                ),
            ]
            + [pl.BlockSpec(memory_space=pl.ANY)] * len(extra),
            out_specs=[
                pl.BlockSpec((block, columns), base_map),
                pl.BlockSpec((8, TILE), lambda i, f, s: (0, 0)),
            ],
        ),
        input_output_aliases=aliases,
        cost_estimate=pl.CostEstimate(
            flops=6 * slices * slice_rows * PW * columns,
            bytes_accessed=8 * slices * slice_rows * columns,
            transcendentals=0,
        ),
        compiler_params=compiler_params(("arbitrary",)),
        name="update_rows",
    )(flags, slice_ids, base, codes, codes, high, low, upper, *extra)


def gate(x, *earlier):
    anywhere = pl.BlockSpec(memory_space=pl.ANY)
    return pl.pallas_call(
        lambda *refs: None,
        out_shape=jax.ShapeDtypeStruct(x.shape, x.dtype),
        in_specs=[anywhere] * (1 + len(earlier)),
        out_specs=anywhere,
        input_output_aliases={0: 0},
        cost_estimate=pl.CostEstimate(flops=0, bytes_accessed=0, transcendentals=0),
        name="gate",
    )(x, *earlier)


def ring_order(count):
    return list(range(0, count, 2)) + list(range(count - 1, 0, -2))


def ring_gather(own, axis, before=()):
    count = lax.axis_size(axis)
    order = ring_order(count)
    ahead = [(order[i], order[(i + 1) % count]) for i in range(count)]
    back = [(b, a) for a, b in ahead]
    place = {d: p for p, d in enumerate(order)}
    steps = [0] + [s for t in range(1, count // 2) for s in (-t, t)] + [count // 2]
    whose = jnp.array([[order[(place[d] + s) % count] for s in steps] for d in range(count)], I32)
    whose = lax.dynamic_index_in_dim(whose, lax.axis_index(axis), keepdims=False)
    pieces = [own]
    left = right = own
    for step in range(1, count // 2):
        if step in before:
            left = gate(left, before[step])
        left, right = lax.ppermute(left, axis, ahead), lax.ppermute(right, axis, back)
        pieces += [left, right]
    half = own.shape[0] // 2
    if count // 2 in before:
        left = gate(left, before[count // 2])
    pieces.append(
        jnp.concatenate([lax.ppermute(left[:half], axis, ahead), lax.ppermute(right[half:], axis, back)], 0)
    )
    return pieces, whose


def scatter_first(parts, axis, before=()):
    count = lax.axis_size(axis)
    index = lax.axis_index(axis)
    odd = lax.ppermute(jnp.concatenate([parts[k : k + 1] for k in range(1, count, 2)]), axis, [(0, 1)])
    if before:
        odd = gate(odd, *before)
    sent = [lax.ppermute(parts[k], axis, [(0, k)]) for k in range(2, count, 2)]
    sent += [lax.ppermute(odd[k // 2], axis, [(1, k)]) for k in range(3, count, 2)]
    mine = jnp.where(index == 0, parts[0], odd[0])
    for x in sent:
        mine = mine + x
    return mine


def tree_broadcast(block, axis):
    count = lax.axis_size(axis)
    index = lax.axis_index(axis)
    reach = count // 2
    while reach >= 1:
        sent = lax.ppermute(block, axis, [(i, i + reach) for i in range(0, count, 2 * reach)])
        block = jnp.where(index % (2 * reach) == reach, sent, block)
        reach //= 2
    return block


def spread_pivots(parent, axis):
    count = lax.axis_size(axis)
    height = PW // count
    mine = parent[:height]
    index = lax.axis_index(axis)
    received = mine
    for k in range(1, count):
        sent = lax.ppermute(parent[k * height : (k + 1) * height], axis, [(0, k)])
        received = jnp.where(index == k, sent, received)
    return received


def gather_pieces(piece, axis):
    count = lax.axis_size(axis)
    pieces, ids = [piece], [lax.axis_index(axis)]
    reach = count // 2
    while reach >= 1:
        pairs = [(i, i ^ reach) for i in range(count)]
        pieces = pieces + [lax.ppermute(x, axis, pairs) for x in pieces]
        ids = ids + [i ^ reach for i in ids]
        reach //= 2
    return pieces, jnp.stack(ids)


def plain_path(flags, parent, child, owner, slot, pivot_inverse):
    bulk_count, column_count = lax.axis_size("bulk"), lax.axis_size("col")
    devices = bulk_count * column_count
    rows, columns = parent.shape
    capacity = max(2, 2 * child.shape[0] // devices)
    width = columns // TILE
    outgoing = pack(owner, slot, child, devices, capacity)
    arrived = lax.all_to_all(outgoing, ("bulk", "col"), split_axis=0, concat_axis=0, tiled=True)
    slots = read_slots(arrived, capacity)
    strip, tile_column = slots // width, slots % width
    pivot_tiles = PW // TILE
    panel_key = jnp.where((slots >= 0) & (tile_column < pivot_tiles), strip * pivot_tiles + tile_column, -1)
    pivot_key = jnp.where((slots >= 0) & (strip < pivot_tiles), slots, -1)

    codes = code_panel(parent, arrived, panel_key, capacity, column_count)
    upper = tree_broadcast(extend(parent, arrived, pivot_key, width, capacity, PW, columns), "bulk")
    high, low, upper = right_factor(flags, jnp.zeros((1,), I32), pivot_inverse, [upper])
    pieces, whose = ring_gather(scatter_first(codes, "col"), "col")
    extended = extend(parent, arrived, slots, width, capacity, rows, columns)
    return update_rows(flags, whose, extended, jnp.stack(pieces), high, low, upper, into=extended)[0]


def quick_path(plan, flags, parent, child, owner, slot, pivot_inverse):
    bulk_count, column_count = lax.axis_size("bulk"), lax.axis_size("col")
    width, half, groups, share = plan["width"], plan["half"], plan["groups"], plan["early"]
    swap = [(i, i ^ half) for i in range(column_count)]
    halves = [
        [b * column_count + h * half + c for b in range(bulk_count) for c in range(half)] for h in range(2)
    ]

    def exchange(blocks, groups=None):
        return lax.all_to_all(
            blocks, ("bulk", "col"), split_axis=0, concat_axis=0, axis_index_groups=groups, tiled=True
        )

    early, near, far, over = sort_children(plan, owner, slot, flags, child)
    early = exchange(early)
    code = scatter_first(encode_panel(parent, column_count), "col")
    pivots = spread_pivots(parent, "bulk")
    early = gate(early, code, pivots)

    codes = read_slots(early, share)
    panel_key = jnp.where((codes >= plan["panel_code"]) & (codes < plan["pivot_code"]), codes - plan["panel_code"], -1)
    pivot_key = jnp.where(codes >= plan["pivot_code"], codes - plan["pivot_code"], -1)
    plain_key = jnp.where(codes < plan["panel_code"], codes, -1)
    code = extend_slice(code, early, panel_key, share)
    pivots = extend(pivots, early, pivot_key, width, share, *pivots.shape)
    uppers, ids = gather_pieces(pivots, "bulk")
    high, low, upper = right_factor(flags, ids, pivot_inverse, uppers)
    far = lax.ppermute(far, "col", swap)
    pieces, whose = ring_gather(code, "col", {2: far})
    cut = len(pieces) - 3
    late = distribute([near, far], over, groups, plan["late"])
    late = exchange(gate(late, high, *pieces[-3:]), halves)
    result, _ = update_rows(flags, whose[:cut], parent, jnp.stack(pieces[:cut]), high, low, upper)
    result, _ = update_rows(flags, whose[cut:], parent, jnp.stack(pieces[cut:]), high, low, upper, into=result)
    result = touch_tiles(result, early, plain_key, width, share)

    over = jnp.full((8, TILE), read_over(late, plan["late"]), I32)
    over = jnp.max(jnp.maximum(over, lax.ppermute(over, "col", swap)))
    return touch_tiles(result, late, read_slots(late, plan["late"]), width, plan["late"]), over


def make_plan(bulk_count, column_count, rows, columns, child_count):
    strips, width, pivot = rows // TILE, columns // TILE, PW // TILE
    if pivot % bulk_count or strips % column_count or column_count % 4:
        return None
    half = column_count // 2
    share = child_count // 2
    panel_strips, pivot_strips = strips // column_count, pivot // bulk_count
    panel_code = strips * width
    return dict(
        devices=bulk_count * column_count,
        columns=column_count,
        width=width,
        pivot=pivot,
        half=half,
        groups=bulk_count * half,
        early=max(2, child_count // (bulk_count * column_count)),
        listed=max(8, share * 7 // 16),
        late=12,
        panel_strips=panel_strips,
        pivot_strips=pivot_strips,
        panel_code=panel_code,
        pivot_code=panel_code + panel_strips * pivot,
    )


def per_device(parent, child, owner, slot, pivot_inverse):
    flags = jnp.stack([lax.axis_index("bulk"), lax.axis_index("col")]).astype(I32)
    owner = owner[:, 0]
    plan = make_plan(
        lax.axis_size("bulk"), lax.axis_size("col"), parent.shape[0], parent.shape[1], child.shape[0]
    )
    if plan is None:
        return plain_path(flags, parent, child, owner, slot, pivot_inverse)
    result, over = quick_path(plan, flags, parent, child, owner, slot, pivot_inverse)

    def again(state):
        return jnp.int32(0), plain_path(flags, parent, child, owner, slot, pivot_inverse)

    return lax.while_loop(lambda state: state[0] > 0, again, (over, result))[1]


def solution(mesh):
    in_specs = (
        P("bulk", "col"),
        P(("bulk", "col"), None, None),
        P(("bulk", "col"), None),
        P(("bulk", "col")),
        P(),
    )
    return jax.shard_map(
        per_device, mesh=mesh, in_specs=in_specs, out_specs=P("bulk", "col"), check_vma=False
    )
```

```python
import functools

import jax
import jax.numpy as jnp
from jax import lax
from jax.experimental import pallas as pl
from jax.experimental.pallas import tpu as pltpu
from jax.sharding import PartitionSpec as P

PW = 512
TILE = 128
META = 16
CODE_TOP = 32600.0
VMEM_LIMIT = 56 * 1024 * 1024

SHORT = pl.CostEstimate(flops=0, bytes_accessed=4096, transcendentals=0)

F32 = jnp.float32
BF16 = jnp.bfloat16
I32 = jnp.int32


def compiler_params(semantics=None):
    return pltpu.CompilerParams(dimension_semantics=semantics, vmem_limit_bytes=VMEM_LIMIT)


def pack_kernel(devices, capacity, owner_ref, slot_ref, child_ref, out_ref, filled, slots, meta, sem, meta_sem):
    child_count = owner_ref.shape[0]

    def clear(d, _):
        filled[d] = 0
        return 0

    lax.fori_loop(0, devices, clear, 0)

    def clear_slot(i, _):
        slots[i] = -1
        return 0

    lax.fori_loop(0, devices * capacity, clear_slot, 0)

    def place(i, _):
        d = owner_ref[i]
        k = filled[d]
        filled[d] = k + 1
        slots[d * capacity + k] = slot_ref[i]
        pltpu.make_async_copy(
            child_ref.at[i], out_ref.at[d, pl.ds(pl.multiple_of(k * TILE, TILE), TILE)], sem
        ).start()
        return 0

    lax.fori_loop(0, child_count, place, 0)
    lane = lax.broadcasted_iota(I32, (META, TILE), 1)
    row = lax.broadcasted_iota(I32, (META, TILE), 0)

    def write_meta(d, _):
        value = jnp.full((META, TILE), -1, I32)
        for k in range(capacity):
            value = jnp.where(lane == k, slots[d * capacity + k], value)
        coded = jnp.where(row == 0, value >> 4, value & 15)
        meta[d] = coded.astype(F32).astype(BF16)
        return 0

    lax.fori_loop(0, devices, write_meta, 0)
    copy = pltpu.make_async_copy(meta, out_ref.at[:, pl.ds(capacity * TILE, META)], meta_sem)
    copy.start()
    pltpu.make_async_copy(child_ref, child_ref, sem).wait()
    copy.wait()


def pack(owner, slot, child, devices, capacity):
    rows = capacity * TILE + META
    return pl.pallas_call(
        functools.partial(pack_kernel, devices, capacity),
        out_shape=jax.ShapeDtypeStruct((devices, rows, TILE), BF16),
        in_specs=[
            pl.BlockSpec(memory_space=pltpu.SMEM),
            pl.BlockSpec(memory_space=pltpu.SMEM),
            pl.BlockSpec(memory_space=pltpu.VMEM),
        ],
        out_specs=pl.BlockSpec(memory_space=pl.ANY),
        scratch_shapes=[
            pltpu.SMEM((devices,), I32),
            pltpu.SMEM((devices * capacity,), I32),
            pltpu.VMEM((devices, META, TILE), BF16),
            pltpu.SemaphoreType.DMA,
            pltpu.SemaphoreType.DMA,
        ],
        compiler_params=compiler_params(),
        name="pack_children",
    )(owner, slot, child)


def lanes(values, count, fallback=-1):
    lane = lax.broadcasted_iota(I32, (META, TILE), 1)
    out = jnp.full((META, TILE), fallback, I32)
    for k in range(count):
        out = jnp.where(lane == k, values(k), out)
    return out


def coded_lines(code, third):
    row = lax.broadcasted_iota(I32, (META, TILE), 0)
    lines = jnp.where(row == 0, code >> 4, jnp.where(row == 1, code & 15, third))
    return lines.astype(F32).astype(BF16)


def fill(ref, count, value):
    def step(i, _):
        ref[i] = value
        return 0

    lax.fori_loop(0, count, step, 0, unroll=8 if count % 8 == 0 else 1)


def sort_kernel(
    plan, kind_ref, dest_ref, code_ref, child_ref,
    early_ref, near_ref, far_ref, over_ref,
    filled, early_code, list_code, list_dest, early_meta, list_meta, sem, meta_sem,
):
    devices, share, size, half = plan["devices"], plan["early"], plan["listed"], plan["half"]
    columns = plan["columns"]
    lists = (near_ref, far_ref)
    fill(filled, devices + 2, 0)
    fill(early_code, devices * share, -1)
    fill(list_code, 2 * size, -1)
    fill(list_dest, 2 * size, -1)
    over_ref[0] = 0

    def send_early(i, dest, k):
        early_code[dest * share + k] = code_ref[i]
        rows = pl.ds(pl.multiple_of(k * TILE, TILE), TILE)
        pltpu.make_async_copy(child_ref.at[i], early_ref.at[dest, rows], sem).start()

    def place_special(i, _):
        @pl.when(kind_ref[i] == 2)
        def _():
            dest = dest_ref[i]
            k = filled[dest]
            filled[dest] = k + 1

            @pl.when(k >= share)
            def _():
                over_ref[0] = 1

            send_early(i, dest, jnp.minimum(k, share - 1))

        return 0

    def place_plain(i, _):
        kind, dest = kind_ref[i], dest_ref[i]

        @pl.when(kind < 2)
        def _():
            k = filled[dest]
            filled[dest] = k + 1

            @pl.when(k < share)
            def _():
                send_early(i, dest, k)

            @pl.when(k >= share)
            def _():
                spot = filled[devices + kind]
                filled[devices + kind] = spot + 1

                @pl.when(spot >= size)
                def _():
                    over_ref[0] = 1

                spot = jnp.minimum(spot, size - 1)
                list_code[kind * size + spot] = code_ref[i]
                list_dest[kind * size + spot] = (dest // columns) * half + lax.rem(dest, half)
                rows = pl.ds(pl.multiple_of(spot * TILE, TILE), TILE)
                for which in range(2):

                    @pl.when(kind == which)
                    def _(which=which):
                        pltpu.make_async_copy(child_ref.at[i], lists[which].at[rows], sem).start()

        return 0

    lax.fori_loop(0, kind_ref.shape[0], place_special, 0)
    lax.fori_loop(0, kind_ref.shape[0], place_plain, 0)
    copies = []
    for which in range(2):
        code = lanes(lambda k: list_code[which * size + k], size)
        dest = lanes(lambda k: list_dest[which * size + k], size)
        list_meta[which] = coded_lines(code, dest)
        copies.append(
            pltpu.make_async_copy(
                list_meta.at[which], lists[which].at[pl.ds(size * TILE, META)], meta_sem.at[which]
            )
        )
        copies[-1].start()

    def write_meta(d, _):
        early_meta[d] = coded_lines(lanes(lambda k: early_code[d * share + k], share), 0)
        return 0

    lax.fori_loop(0, devices, write_meta, 0)
    copies.append(
        pltpu.make_async_copy(early_meta, early_ref.at[:, pl.ds(share * TILE, META)], meta_sem.at[2])
    )
    copies[-1].start()
    pltpu.make_async_copy(child_ref, child_ref, sem).wait()
    for copy in copies:
        copy.wait()


def sort_children(plan, owner, slot, flags, child):
    devices, share, listed = plan["devices"], plan["early"], plan["listed"]
    bulk, col = owner // plan["columns"], owner % plan["columns"]
    strip, tile = slot // plan["width"], slot % plan["width"]
    pivot = (bulk == 0) & (strip < plan["pivot"])
    panel = (col == 0) & (tile < plan["pivot"])
    pivot, panel = pivot & ~panel, panel & ~pivot
    bulk = jnp.where(pivot, strip // plan["pivot_strips"], bulk)
    col = jnp.where(panel, strip // plan["panel_strips"], col)
    code = jnp.where(panel, plan["panel_code"] + (strip % plan["panel_strips"]) * plan["pivot"] + tile, slot)
    code = jnp.where(pivot, plan["pivot_code"] + (strip % plan["pivot_strips"]) * plan["width"] + tile, code)
    here = col // plan["half"] == flags[1] // plan["half"]
    kind = jnp.where(pivot | panel, 2, jnp.where(here, 0, 1))
    dest = bulk * plan["columns"] + col
    anywhere = pl.BlockSpec(memory_space=pl.ANY)
    scalars = pl.BlockSpec(memory_space=pltpu.SMEM)
    in_list = jax.ShapeDtypeStruct((listed * TILE + META, TILE), BF16)
    return pl.pallas_call(
        functools.partial(sort_kernel, plan),
        out_shape=[
            jax.ShapeDtypeStruct((devices, share * TILE + META, TILE), BF16),
            in_list,
            in_list,
            jax.ShapeDtypeStruct((1,), I32),
        ],
        in_specs=[scalars, scalars, scalars, pl.BlockSpec(memory_space=pltpu.VMEM)],
        out_specs=[anywhere, anywhere, anywhere, scalars],
        scratch_shapes=[
            pltpu.SMEM((devices + 2,), I32),
            pltpu.SMEM((devices * share,), I32),
            pltpu.SMEM((2 * listed,), I32),
            pltpu.SMEM((2 * listed,), I32),
            pltpu.VMEM((devices, META, TILE), BF16),
            pltpu.VMEM((2, META, TILE), BF16),
            pltpu.SemaphoreType.DMA,
            pltpu.SemaphoreType.DMA((3,)),
        ],
        compiler_params=compiler_params(),
        cost_estimate=SHORT,
        name="sort_children",
    )(kind, dest, code, child)


def read_list(listed):
    count = (listed.shape[0] - META) // TILE
    lines = listed[count * TILE : count * TILE + 3, :count].astype(I32)
    return lines[0] * 16 + lines[1], lines[2]


def distribute_kernel(groups, capacity, sizes, *refs):
    n = len(sizes)
    code_refs, dest_refs, block_refs = refs[:n], refs[n : 2 * n], refs[2 * n : 3 * n]
    over_in, out_ref, over_ref, filled, codes, meta, spare, sem, meta_sem = refs[3 * n :]
    fill(filled, groups, 0)
    fill(codes, groups * capacity, -1)
    over_ref[0] = over_in[0]
    for code_ref, dest_ref, block_ref, size in zip(code_refs, dest_refs, block_refs, sizes):

        def place(i, _, code_ref=code_ref, dest_ref=dest_ref, block_ref=block_ref):
            dest = dest_ref[i]
            block = block_ref.at[pl.ds(pl.multiple_of(i * TILE, TILE), TILE)]

            @pl.when(dest >= 0)
            def _():
                k = filled[dest]
                filled[dest] = k + 1

                @pl.when(k >= capacity)
                def _():
                    over_ref[0] = 1

                k = jnp.minimum(k, capacity - 1)
                codes[dest * capacity + k] = code_ref[i]
                pltpu.make_async_copy(
                    block, out_ref.at[dest, pl.ds(pl.multiple_of(k * TILE, TILE), TILE)], sem
                ).start()

            @pl.when(dest < 0)
            def _():
                pltpu.make_async_copy(block, spare, sem).start()

            return 0

        lax.fori_loop(0, size, place, 0)

    def write_meta(g, _):
        meta[g] = coded_lines(lanes(lambda k: codes[g * capacity + k], capacity), over_ref[0])
        return 0

    lax.fori_loop(0, groups, write_meta, 0)
    copy = pltpu.make_async_copy(meta, out_ref.at[:, pl.ds(capacity * TILE, META)], meta_sem)
    copy.start()
    for block_ref, size in zip(block_refs, sizes):
        blocks = block_ref.at[pl.ds(0, size * TILE)]
        pltpu.make_async_copy(blocks, blocks, sem).wait()
    copy.wait()


def distribute(lists, over, groups, capacity):
    sizes = [(x.shape[0] - META) // TILE for x in lists]
    codes, dests = zip(*[read_list(x) for x in lists])
    n = len(lists)
    return pl.pallas_call(
        functools.partial(distribute_kernel, groups, capacity, sizes),
        out_shape=[
            jax.ShapeDtypeStruct((groups, capacity * TILE + META, TILE), BF16),
            jax.ShapeDtypeStruct((1,), I32),
        ],
        in_specs=[pl.BlockSpec(memory_space=pltpu.SMEM)] * (2 * n)
        + [pl.BlockSpec(memory_space=pltpu.VMEM)] * n
        + [pl.BlockSpec(memory_space=pltpu.SMEM)],
        out_specs=[pl.BlockSpec(memory_space=pl.ANY), pl.BlockSpec(memory_space=pltpu.SMEM)],
        scratch_shapes=[
            pltpu.SMEM((groups,), I32),
            pltpu.SMEM((groups * capacity,), I32),
            pltpu.VMEM((groups, META, TILE), BF16),
            pltpu.VMEM((TILE, TILE), BF16),
            pltpu.SemaphoreType.DMA,
            pltpu.SemaphoreType.DMA,
        ],
        compiler_params=compiler_params(),
        cost_estimate=SHORT,
        name="distribute",
    )(*codes, *dests, *lists, over)[0]


def read_over(arrived, capacity):
    return jnp.max(arrived[:, capacity * TILE + 2, 0].astype(I32))


def read_slots(arrived, capacity):
    coded = arrived[:, capacity * TILE : capacity * TILE + 2, :capacity].astype(I32)
    return (coded[:, 0] * 16 + coded[:, 1]).reshape(-1)


def build_lists(key_ref, head, following, width):
    def clear(i, _):
        head[i] = -1
        return 0

    lax.fori_loop(0, head.shape[0], clear, 0)

    def add(i, _):
        key = key_ref[i]

        @pl.when(key >= 0)
        def _():
            strip = key // width
            following[i] = head[strip]
            head[strip] = i

        return 0

    lax.fori_loop(0, key_ref.shape[0], add, 0)


def add_strip(key_ref, arrived_ref, out, head, following, strip, width, capacity, row):
    def body(i):
        column = pl.multiple_of((key_ref[i] % width) * TILE, TILE)
        start = pl.multiple_of((i % capacity) * TILE, TILE)
        block = arrived_ref[i // capacity, pl.ds(start, TILE), :]
        spot = (pl.ds(row, TILE), pl.ds(column, TILE))
        out[spot] = out[spot] + block.astype(F32)
        return following[i]

    lax.while_loop(lambda i: i >= 0, body, head[strip])


def extend_kernel(width, capacity, key_ref, base_ref, arrived_ref, out_ref, head, following):
    step = pl.program_id(0)

    @pl.when(step == 0)
    def _():
        build_lists(key_ref, head, following, width)

    out_ref[...] = base_ref[...]
    strips = base_ref.shape[0] // TILE
    for s in range(strips):
        add_strip(
            key_ref, arrived_ref, out_ref, head, following, step * strips + s, width, capacity, s * TILE
        )


def extend(base, arrived, key, width, capacity, rows, columns):
    return pl.pallas_call(
        functools.partial(extend_kernel, width, capacity),
        out_shape=jax.ShapeDtypeStruct((rows, columns), F32),
        grid_spec=pltpu.PrefetchScalarGridSpec(
            num_scalar_prefetch=1,
            grid=(rows // TILE,),
            in_specs=[
                pl.BlockSpec((TILE, columns), lambda i, k: (i, 0)),
                pl.BlockSpec(memory_space=pltpu.VMEM),
            ],
            out_specs=pl.BlockSpec((TILE, columns), lambda i, k: (i, 0)),
            scratch_shapes=[
                pltpu.SMEM((rows // TILE,), I32),
                pltpu.SMEM((key.shape[0],), I32),
            ],
        ),
        compiler_params=compiler_params(("arbitrary",)),
        cost_estimate=pl.CostEstimate(flops=rows * columns, bytes_accessed=12 * rows * columns, transcendentals=0),
        name="extend_add",
    )(key, base, arrived)


AHEAD = 24
BUFFERS = 48


def touch_kernel(
    width, capacity, key_ref, base_ref, arrived_ref, out_ref,
    tiles, head, following, active, read_sem, write_sem,
):
    del base_ref
    fill(head, head.shape[0], -1)

    def chain(i, count):
        key = key_ref[i]
        at = jnp.maximum(key, 0)
        first = jnp.logical_and(key >= 0, head[at] < 0)

        @pl.when(key >= 0)
        def _():
            following[i] = head[at]
            head[at] = i

        @pl.when(first)
        def _():
            active[count] = key

        return count + first.astype(I32)

    count = lax.fori_loop(0, key_ref.shape[0], chain, jnp.int32(0))

    def copy(j, out):
        key = active[j]
        slot = lax.rem(j, BUFFERS)
        place = out_ref.at[
            pl.ds(pl.multiple_of((key // width) * TILE, TILE), TILE),
            pl.ds(pl.multiple_of((key % width) * TILE, TILE), TILE),
        ]
        if out:
            return pltpu.make_async_copy(tiles.at[slot], place, write_sem.at[slot])
        return pltpu.make_async_copy(place, tiles.at[slot], read_sem.at[slot])

    def first_reads(j, _):
        copy(j, False).start()
        return 0

    lax.fori_loop(0, jnp.minimum(count, AHEAD), first_reads, 0)

    def step(j, _):
        later = j + AHEAD

        @pl.when(later < count)
        def _():
            @pl.when(later >= BUFFERS)
            def _():
                copy(later - BUFFERS, True).wait()

            copy(later, False).start()

        copy(j, False).wait()
        slot = lax.rem(j, BUFFERS)

        def body(i):
            start = pl.multiple_of((i % capacity) * TILE, TILE)
            tiles[slot] = tiles[slot] + arrived_ref[i // capacity, pl.ds(start, TILE), :].astype(F32)
            return following[i]

        lax.while_loop(lambda i: i >= 0, body, head[active[j]])
        copy(j, True).start()
        return 0

    lax.fori_loop(0, count, step, 0)

    def last_writes(j, _):
        copy(j, True).wait()
        return 0

    lax.fori_loop(jnp.maximum(count - BUFFERS, 0), count, last_writes, 0)


def touch_tiles(base, arrived, key, width, capacity):
    rows, columns = base.shape
    return pl.pallas_call(
        functools.partial(touch_kernel, width, capacity),
        out_shape=jax.ShapeDtypeStruct((rows, columns), F32),
        in_specs=[
            pl.BlockSpec(memory_space=pltpu.SMEM),
            pl.BlockSpec(memory_space=pl.ANY),
            pl.BlockSpec(memory_space=pltpu.VMEM),
        ],
        out_specs=pl.BlockSpec(memory_space=pl.ANY),
        scratch_shapes=[
            pltpu.VMEM((BUFFERS, TILE, TILE), F32),
            pltpu.SMEM((rows * columns // (TILE * TILE),), I32),
            pltpu.SMEM((key.shape[0],), I32),
            pltpu.SMEM((key.shape[0],), I32),
            pltpu.SemaphoreType.DMA((BUFFERS,)),
            pltpu.SemaphoreType.DMA((BUFFERS,)),
        ],
        input_output_aliases={1: 0},
        compiler_params=compiler_params(),
        name="touch_tiles",
    )(key, base, arrived)


def code_rows(values):
    top = jnp.maximum(jnp.max(jnp.abs(values), axis=1, keepdims=True), 1e-30)
    exponent = jnp.ceil(jnp.log2(top) * 64.0)
    code = jnp.round(values * (CODE_TOP * jnp.exp2(exponent * (-1.0 / 64.0))))
    return code.astype(I32), exponent


def diagonal(n):
    return lax.broadcasted_iota(I32, (n, n), 0) == lax.broadcasted_iota(I32, (n, n), 1)


def write_code(out_ref, lead, values, rows, s):
    code, exponent = code_rows(values)
    out_ref[(*lead, pl.ds(s * TILE, TILE), slice(None))] = code.astype(jnp.int16)
    line = jnp.sum(jnp.where(diagonal(TILE), exponent, 0.0), axis=0, keepdims=True)
    out_ref[(*lead, pl.ds(rows, META), pl.ds(s * TILE, TILE))] = (
        jnp.broadcast_to(line, (META, TILE)).astype(I32).astype(jnp.int16)
    )


def row_scale(lines):
    line = lines.astype(I32).astype(F32)[:1]
    exponent = jnp.sum(jnp.where(diagonal(TILE), line, 0.0), axis=1, keepdims=True)
    return jnp.exp2(exponent * (1.0 / 64.0)) * (1.0 / CODE_TOP)


def encode_kernel(base_ref, out_ref):
    rows = base_ref.shape[0]
    out_ref[0, pl.ds(rows, META), :] = jnp.zeros((META, out_ref.shape[2]), jnp.int16)
    for s in range(rows // TILE):
        write_code(out_ref, (0,), base_ref[pl.ds(s * TILE, TILE), :], rows, s)


def encode_panel(base, slices):
    rows = base.shape[0] // slices
    return pl.pallas_call(
        encode_kernel,
        out_shape=jax.ShapeDtypeStruct((slices, rows + META, PW), jnp.int16),
        grid=(slices,),
        in_specs=[pl.BlockSpec((rows, PW), lambda i: (i, 0))],
        out_specs=pl.BlockSpec((1, rows + META, PW), lambda i: (i, 0, 0)),
        compiler_params=compiler_params(("arbitrary",)),
        cost_estimate=SHORT,
        name="encode_panel",
    )(base)


def slice_kernel(width, capacity, key_ref, code_ref, arrived_ref, out_ref, work, head, following):
    build_lists(key_ref, head, following, width)
    rows = work.shape[0]
    out_ref[pl.ds(rows, META), :] = jnp.zeros((META, out_ref.shape[1]), jnp.int16)
    for s in range(rows // TILE):
        spot = pl.ds(s * TILE, TILE)
        work[spot, :] = code_ref[spot, :].astype(I32).astype(F32) * row_scale(
            code_ref[pl.ds(rows, META), spot]
        )
        add_strip(key_ref, arrived_ref, work, head, following, s, width, capacity, s * TILE)
        write_code(out_ref, (), work[spot, :], rows, s)


def extend_slice(code, arrived, key, capacity):
    rows = code.shape[0] - META
    return pl.pallas_call(
        functools.partial(slice_kernel, PW // TILE, capacity),
        out_shape=jax.ShapeDtypeStruct(code.shape, jnp.int16),
        in_specs=[
            pl.BlockSpec(memory_space=pltpu.SMEM),
            pl.BlockSpec(memory_space=pltpu.VMEM),
            pl.BlockSpec(memory_space=pltpu.VMEM),
        ],
        out_specs=pl.BlockSpec(memory_space=pltpu.VMEM),
        scratch_shapes=[
            pltpu.VMEM((rows, PW), F32),
            pltpu.SMEM((rows // TILE,), I32),
            pltpu.SMEM((key.shape[0],), I32),
        ],
        compiler_params=compiler_params(),
        cost_estimate=SHORT,
        name="extend_slice",
    )(key, code, arrived)


def panel_kernel(width, capacity, key_ref, base_ref, arrived_ref, out_ref, work, head, following):
    step = pl.program_id(0)

    @pl.when(step == 0)
    def _():
        build_lists(key_ref, head, following, width)

    work[...] = base_ref[...]
    rows = base_ref.shape[0]
    strips = rows // TILE
    out_ref[0, pl.ds(rows, META), :] = jnp.zeros((META, out_ref.shape[2]), jnp.int16)
    for s in range(strips):
        add_strip(
            key_ref, arrived_ref, work, head, following, step * strips + s, width, capacity, s * TILE
        )
        write_code(out_ref, (0,), work[pl.ds(s * TILE, TILE), :], rows, s)


def code_panel(base, arrived, key, capacity, slices):
    rows = base.shape[0] // slices
    width = PW // TILE
    return pl.pallas_call(
        functools.partial(panel_kernel, width, capacity),
        out_shape=jax.ShapeDtypeStruct((slices, rows + META, PW), jnp.int16),
        grid_spec=pltpu.PrefetchScalarGridSpec(
            num_scalar_prefetch=1,
            grid=(slices,),
            in_specs=[
                pl.BlockSpec((rows, PW), lambda i, k: (i, 0)),
                pl.BlockSpec(memory_space=pltpu.VMEM),
            ],
            out_specs=pl.BlockSpec((1, rows + META, PW), lambda i, k: (i, 0, 0)),
            scratch_shapes=[
                pltpu.VMEM((rows, PW), F32),
                pltpu.SMEM((base.shape[0] // TILE,), I32),
                pltpu.SMEM((key.shape[0],), I32),
            ],
        ),
        compiler_params=compiler_params(("arbitrary",)),
        name="code_panel",
    )(key, base, arrived)


def split(x):
    high = x.astype(BF16)
    return high, (x - high.astype(F32)).astype(BF16)


def right_kernel(flag_ref, id_ref, pivot_ref, *refs):
    pieces, (high_ref, low_ref, upper_ref) = refs[:-3], refs[-3:]
    step = pl.program_id(0)
    height, columns = pieces[0].shape
    for p, piece in enumerate(pieces):
        upper_ref[pl.ds(pl.multiple_of(id_ref[p] * height, 8), height), :] = piece[...]
    row = lax.broadcasted_iota(I32, (PW, columns), 0)
    column = lax.broadcasted_iota(I32, (PW, columns), 1) + step * columns
    in_panel = jnp.logical_and(column < PW, flag_ref[1] == 0)
    upper = jnp.where(in_panel, jnp.where(row == column, -1.0, 0.0), upper_ref[...])
    a, b = split(pivot_ref[...])
    c, d = split(upper)
    right = (
        jnp.dot(a, d, preferred_element_type=F32) + jnp.dot(b, c, preferred_element_type=F32)
    ) + jnp.dot(a, c, preferred_element_type=F32)
    high_ref[...], low_ref[...] = split(right)


def right_factor(flags, ids, pivot_inverse, pieces):
    height, columns = pieces[0].shape
    block = min(512, columns)
    spec = pl.BlockSpec((PW, block), lambda i, f, s: (0, i))
    return pl.pallas_call(
        right_kernel,
        out_shape=[jax.ShapeDtypeStruct((PW, columns), t) for t in (BF16, BF16, F32)],
        grid_spec=pltpu.PrefetchScalarGridSpec(
            num_scalar_prefetch=2,
            grid=(columns // block,),
            in_specs=[pl.BlockSpec((PW, PW), lambda i, f, s: (0, 0))]
            + [pl.BlockSpec((height, block), lambda i, f, s: (0, i))] * len(pieces),
            out_specs=[spec, spec, spec],
        ),
        compiler_params=compiler_params(("arbitrary",)),
        cost_estimate=SHORT,
        name="right_factor",
    )(flags, ids, pivot_inverse, *pieces)


def update_kernel(block, per_slice, flag_ref, slice_ref, base_ref, code_ref, scale_ref, high_ref, low_ref, upper_ref, *refs):
    out_ref, token_ref = refs[-2:]
    step = pl.program_id(0)

    @pl.when(step == 0)
    def _():
        token_ref[...] = jnp.zeros_like(token_ref)

    row_block = slice_ref[step // per_slice] * per_slice + lax.rem(step, per_slice)
    above = jnp.logical_and(flag_ref[0] == 0, row_block < PW // block)

    @pl.when(above)
    def _():
        out_ref[:, pl.ds(PW, out_ref.shape[1] - PW)] = upper_ref[:, pl.ds(PW, out_ref.shape[1] - PW)]
        out_ref[:, pl.ds(0, PW)] = jnp.where(flag_ref[1] == 0, base_ref[:, pl.ds(0, PW)], upper_ref[:, pl.ds(0, PW)])

    @pl.when(jnp.logical_not(above))
    def _():
        code = code_ref[0].astype(I32)
        upper_part = (code + 128) >> 8
        lower_part = (code - upper_part * 256).astype(F32).astype(BF16)
        upper_part = (upper_part * 256).astype(F32).astype(BF16)
        high, low = high_ref[...], low_ref[...]
        product = (
            jnp.dot(lower_part, high, preferred_element_type=F32)
            + jnp.dot(upper_part, low, preferred_element_type=F32)
        ) + jnp.dot(upper_part, high, preferred_element_type=F32)
        for s in range(block // TILE):
            scale = row_scale(scale_ref[0, :, pl.ds(s * TILE, TILE)])
            rows = slice(s * TILE, (s + 1) * TILE)
            update = scale * product[rows]
            out_ref[pl.ds(s * TILE, TILE), pl.ds(PW, out_ref.shape[1] - PW)] = (
                base_ref[pl.ds(s * TILE, TILE), pl.ds(PW, out_ref.shape[1] - PW)] - update[:, PW:]
            )
            kept = jnp.where(flag_ref[1] == 0, 0.0, 1.0)
            out_ref[pl.ds(s * TILE, TILE), pl.ds(0, PW)] = (
                base_ref[pl.ds(s * TILE, TILE), pl.ds(0, PW)] * kept - update[:, :PW]
            )


def update_rows(flags, slice_ids, base, codes, high, low, upper, into=None):
    rows, columns = base.shape
    slices, slice_rows, _ = codes.shape
    slice_rows -= META
    block = min(256, slice_rows)
    per_slice = slice_rows // block

    if into is None:
        extra, aliases = [], {}
    elif into is base:
        extra, aliases = [], {2: 0}
    else:
        extra, aliases = [into], {8: 0}

    def base_map(i, f, s):
        return (s[i // per_slice] * per_slice + lax.rem(i, per_slice), 0)

    return pl.pallas_call(
        functools.partial(update_kernel, block, per_slice),
        out_shape=[jax.ShapeDtypeStruct((rows, columns), F32), jax.ShapeDtypeStruct((8, TILE), F32)],
        grid_spec=pltpu.PrefetchScalarGridSpec(
            num_scalar_prefetch=2,
            grid=(slices * per_slice,),
            in_specs=[
                pl.BlockSpec((block, columns), base_map),
                pl.BlockSpec((1, block, PW), lambda i, f, s: (i // per_slice, lax.rem(i, per_slice), 0)),
                pl.BlockSpec(
                    (1, META, block),
                    lambda i, f, s: (i // per_slice, slice_rows // META, lax.rem(i, per_slice)),
                ),
                pl.BlockSpec((PW, columns), lambda i, f, s: (0, 0)),
                pl.BlockSpec((PW, columns), lambda i, f, s: (0, 0)),
                pl.BlockSpec(
                    (block, columns), lambda i, f, s: (jnp.minimum(base_map(i, f, s)[0], PW // block - 1), 0)
                ),
            ]
            + [pl.BlockSpec(memory_space=pl.ANY)] * len(extra),
            out_specs=[
                pl.BlockSpec((block, columns), base_map),
                pl.BlockSpec((8, TILE), lambda i, f, s: (0, 0)),
            ],
        ),
        input_output_aliases=aliases,
        cost_estimate=pl.CostEstimate(
            flops=6 * slices * slice_rows * PW * columns,
            bytes_accessed=8 * slices * slice_rows * columns,
            transcendentals=0,
        ),
        compiler_params=compiler_params(("arbitrary",)),
        name="update_rows",
    )(flags, slice_ids, base, codes, codes, high, low, upper, *extra)


def gate(x, *earlier):
    anywhere = pl.BlockSpec(memory_space=pl.ANY)
    return pl.pallas_call(
        lambda *refs: None,
        out_shape=jax.ShapeDtypeStruct(x.shape, x.dtype),
        in_specs=[anywhere] * (1 + len(earlier)),
        out_specs=anywhere,
        input_output_aliases={0: 0},
        cost_estimate=pl.CostEstimate(flops=0, bytes_accessed=0, transcendentals=0),
        name="gate",
    )(x, *earlier)


def ring_order(count):
    return list(range(0, count, 2)) + list(range(count - 1, 0, -2))


def ring_gather(own, axis, before=()):
    count = lax.axis_size(axis)
    order = ring_order(count)
    ahead = [(order[i], order[(i + 1) % count]) for i in range(count)]
    back = [(b, a) for a, b in ahead]
    place = {d: p for p, d in enumerate(order)}
    steps = [0] + [s for t in range(1, count // 2) for s in (-t, t)] + [count // 2]
    whose = jnp.array([[order[(place[d] + s) % count] for s in steps] for d in range(count)], I32)
    whose = lax.dynamic_index_in_dim(whose, lax.axis_index(axis), keepdims=False)
    pieces = [own]
    left = right = own
    for step in range(1, count // 2):
        if step in before:
            left = gate(left, *before[step])
        left, right = lax.ppermute(left, axis, ahead), lax.ppermute(right, axis, back)
        pieces += [left, right]
    half = own.shape[0] // 2
    if count // 2 in before:
        left = gate(left, *before[count // 2])
    pieces.append(
        jnp.concatenate([lax.ppermute(left[:half], axis, ahead), lax.ppermute(right[half:], axis, back)], 0)
    )
    return pieces, whose


def scatter_first(parts, axis, before=()):
    count = lax.axis_size(axis)
    index = lax.axis_index(axis)
    odd = lax.ppermute(jnp.concatenate([parts[k : k + 1] for k in range(1, count, 2)]), axis, [(0, 1)])
    if before:
        odd = gate(odd, *before)
    sent = [lax.ppermute(parts[k], axis, [(0, k)]) for k in range(2, count, 2)]
    sent += [lax.ppermute(odd[k // 2], axis, [(1, k)]) for k in range(3, count, 2)]
    mine = jnp.where(index == 0, parts[0], odd[0])
    for x in sent:
        mine = mine + x
    return mine


def tree_broadcast(block, axis):
    count = lax.axis_size(axis)
    index = lax.axis_index(axis)
    reach = count // 2
    while reach >= 1:
        sent = lax.ppermute(block, axis, [(i, i + reach) for i in range(0, count, 2 * reach)])
        block = jnp.where(index % (2 * reach) == reach, sent, block)
        reach //= 2
    return block


def spread_pivots(parent, axis):
    count = lax.axis_size(axis)
    height = PW // count
    mine = parent[:height]
    index = lax.axis_index(axis)
    received = mine
    for k in range(1, count):
        sent = lax.ppermute(parent[k * height : (k + 1) * height], axis, [(0, k)])
        received = jnp.where(index == k, sent, received)
    return received


def gather_pieces(piece, axis):
    count = lax.axis_size(axis)
    pieces, ids = [piece], [lax.axis_index(axis)]
    reach = count // 2
    while reach >= 1:
        pairs = [(i, i ^ reach) for i in range(count)]
        pieces = pieces + [lax.ppermute(x, axis, pairs) for x in pieces]
        ids = ids + [i ^ reach for i in ids]
        reach //= 2
    return pieces, jnp.stack(ids)


def plain_path(flags, parent, child, owner, slot, pivot_inverse):
    bulk_count, column_count = lax.axis_size("bulk"), lax.axis_size("col")
    devices = bulk_count * column_count
    rows, columns = parent.shape
    capacity = max(2, 2 * child.shape[0] // devices)
    width = columns // TILE
    outgoing = pack(owner, slot, child, devices, capacity)
    arrived = lax.all_to_all(outgoing, ("bulk", "col"), split_axis=0, concat_axis=0, tiled=True)
    slots = read_slots(arrived, capacity)
    strip, tile_column = slots // width, slots % width
    pivot_tiles = PW // TILE
    panel_key = jnp.where((slots >= 0) & (tile_column < pivot_tiles), strip * pivot_tiles + tile_column, -1)
    pivot_key = jnp.where((slots >= 0) & (strip < pivot_tiles), slots, -1)

    codes = code_panel(parent, arrived, panel_key, capacity, column_count)
    upper = tree_broadcast(extend(parent, arrived, pivot_key, width, capacity, PW, columns), "bulk")
    high, low, upper = right_factor(flags, jnp.zeros((1,), I32), pivot_inverse, [upper])
    pieces, whose = ring_gather(scatter_first(codes, "col"), "col")
    extended = extend(parent, arrived, slots, width, capacity, rows, columns)
    return update_rows(flags, whose, extended, jnp.stack(pieces), high, low, upper, into=extended)[0]


def quick_path(plan, flags, parent, child, owner, slot, pivot_inverse):
    bulk_count, column_count = lax.axis_size("bulk"), lax.axis_size("col")
    width, half, groups, share = plan["width"], plan["half"], plan["groups"], plan["early"]
    swap = [(i, i ^ half) for i in range(column_count)]
    halves = [
        [b * column_count + h * half + c for b in range(bulk_count) for c in range(half)] for h in range(2)
    ]

    def exchange(blocks, groups=None):
        return lax.all_to_all(
            blocks, ("bulk", "col"), split_axis=0, concat_axis=0, axis_index_groups=groups, tiled=True
        )

    early, near, far, over = sort_children(plan, owner, slot, flags, child)
    early = exchange(early)
    code = scatter_first(encode_panel(parent, column_count), "col")
    pivots = spread_pivots(parent, "bulk")
    early = gate(early, code, pivots)

    codes = read_slots(early, share)
    panel_key = jnp.where((codes >= plan["panel_code"]) & (codes < plan["pivot_code"]), codes - plan["panel_code"], -1)
    pivot_key = jnp.where(codes >= plan["pivot_code"], codes - plan["pivot_code"], -1)
    plain_key = jnp.where(codes < plan["panel_code"], codes, -1)
    code = extend_slice(code, early, panel_key, share)
    pivots = extend(pivots, early, pivot_key, width, share, *pivots.shape)
    uppers, ids = gather_pieces(pivots, "bulk")
    high, low, upper = right_factor(flags, ids, pivot_inverse, uppers)
    far = lax.ppermute(far, "col", swap)
    late = distribute([near, far], over, groups, plan["late"])
    pieces, whose = ring_gather(code, "col", {2: [far], column_count // 2 - 1: [late]})
    cut = len(pieces) - 3
    late = exchange(gate(late, *pieces[-3:], *uppers[1:]), halves)
    result, _ = update_rows(flags, whose[:cut], parent, jnp.stack(pieces[:cut]), high, low, upper)
    result, _ = update_rows(flags, whose[cut:], parent, jnp.stack(pieces[cut:]), high, low, upper, into=result)
    result = touch_tiles(result, early, plain_key, width, share)

    over = jnp.full((8, TILE), read_over(late, plan["late"]), I32)
    over = jnp.max(jnp.maximum(over, lax.ppermute(over, "col", swap)))
    return touch_tiles(result, late, read_slots(late, plan["late"]), width, plan["late"]), over


def make_plan(bulk_count, column_count, rows, columns, child_count):
    strips, width, pivot = rows // TILE, columns // TILE, PW // TILE
    if pivot % bulk_count or strips % column_count or column_count % 4:
        return None
    half = column_count // 2
    share = child_count // 2
    panel_strips, pivot_strips = strips // column_count, pivot // bulk_count
    panel_code = strips * width
    return dict(
        devices=bulk_count * column_count,
        columns=column_count,
        width=width,
        pivot=pivot,
        half=half,
        groups=bulk_count * half,
        early=max(2, child_count // (bulk_count * column_count)),
        listed=max(8, share * 7 // 16),
        late=12,
        panel_strips=panel_strips,
        pivot_strips=pivot_strips,
        panel_code=panel_code,
        pivot_code=panel_code + panel_strips * pivot,
    )


def per_device(parent, child, owner, slot, pivot_inverse):
    flags = jnp.stack([lax.axis_index("bulk"), lax.axis_index("col")]).astype(I32)
    owner = owner[:, 0]
    plan = make_plan(
        lax.axis_size("bulk"), lax.axis_size("col"), parent.shape[0], parent.shape[1], child.shape[0]
    )
    if plan is None:
        return plain_path(flags, parent, child, owner, slot, pivot_inverse)
    result, over = quick_path(plan, flags, parent, child, owner, slot, pivot_inverse)

    def again(state):
        return jnp.int32(0), plain_path(flags, parent, child, owner, slot, pivot_inverse)

    return lax.while_loop(lambda state: state[0] > 0, again, (over, result))[1]


def solution(mesh):
    in_specs = (
        P("bulk", "col"),
        P(("bulk", "col"), None, None),
        P(("bulk", "col"), None),
        P(("bulk", "col")),
        P(),
    )
    return jax.shard_map(
        per_device, mesh=mesh, in_specs=in_specs, out_specs=P("bulk", "col"), check_vma=False
    )
```
